256 devices in a mesh: real: 4 (over x), cell: 64 (over z, y, core).
Axes of the slice: x: 4, y: 4, z: 8, core: 2. Of those that a mesh axis runs over, the one named last changes fastest.
Arguments:
- initial: float32 [8, 128, 64, 128], P('real', 'cell'), may hold values from 0 to 2
- velocity: float32 [8, 3, 128, 64, 128], P('real', None, 'cell'), may hold values from -1 to 1
- dispersion: float32 [8, 3, 128, 64, 128], P('real', None, 'cell'), may hold values from 0.05 to 0.5
- bounds: int32 [128, 64], P('cell'), may hold values from 64 to 128
- basis: bfloat16 [256, 128, 64, 128], P(None, 'cell'), may hold values from -0.005859375 to 0.005859375
Outputs:
- mean_field: float32 [128, 64, 128], P('cell')
- spread_field: float32 [128, 64, 128], P('cell')
- coord_mean: float32 [256], replicated
- coord_cov: float32 [256, 256], replicated
The draws below stay inside these ranges and needn't reach their ends.
All inputs are finite; a program needn't handle non-finite values.
Results may differ from the reference program's by a relative error of at most 0.012.
Values sent between devices are 32-bit elements; how exact they have to be, the bound alone decides.
No kernel may reach another device: no remote copies, remote signals or barrier semaphores. Data moves between devices by JAX's collectives and lax.ppermute only.
A program may use at most 64 MiB of HBM per device.

```python
import math
import jax
import jax.numpy as jnp
from jax import lax

NY = 64
NZ = 128
STEPS = 2
PCS = 256
REALS = 8
NX = 128


def place_ends(array, key, low, largest):
    longest = array.shape.index(max(array.shape))
    spots = []
    for shift in (0, 1):
        where = [jax.random.randint(jax.random.fold_in(key, axis), (), 0, length) for axis, length in enumerate(array.shape)]
        where[longest] = (where[longest] + shift) % array.shape[longest]
        spots.append(tuple(where))
    return array.at[spots[0]].set(low).at[spots[1]].set(largest)


def steps_of(key, extent, pieces, least, high):
    level = 1.0
    for dim, blocks in pieces:
        draws = jax.random.uniform(jax.random.fold_in(jax.random.fold_in(key, 6), dim), (blocks,), jnp.float32, least / len(pieces), high / len(pieces))
        level = level * jnp.repeat(jnp.exp(draws), extent[dim] // blocks).reshape((-1,) + (1,) * (len(extent) - 1 - dim))
    return level


def gaussian(key, dims, deviation, bound, pieces=(), held_as=jnp.bfloat16):
    entries = jax.random.normal(key, dims, jnp.float32) * deviation
    if len(pieces) > 0:
        entries = steps_of(key, dims, pieces, -0.22, 0.18) * entries
    return jnp.clip(entries, min=-bound, max=bound).astype(held_as)


def setup_inputs(seed: int = 0) -> dict:
    splits = jax.random.split(jax.random.key(seed), 6)
    initial = jnp.clip(2.0 * jax.random.uniform(splits[0], (REALS, NX, NY, NZ), jnp.float32) ** steps_of(splits[0], (REALS, NX, NY, NZ), ((0, 4), (1, 64)), -0.2, 0.2), 0.0, 2.0)
    velocity = jnp.clip(jax.random.uniform(splits[1], (REALS, 3, NX, NY, NZ), jnp.float32, -1.0, 1.0) * steps_of(splits[1], (REALS, 3, NX, NY, NZ), ((0, 4), (2, 64)), -0.4, 0.0), -1.0, 1.0)
    dispersion = jnp.clip(jnp.exp(math.log(0.5) - 2.3025851 * jax.random.uniform(splits[2], (REALS, 3, NX, NY, NZ), jnp.float32) ** steps_of(splits[2], (REALS, 3, NX, NY, NZ), ((0, 4), (2, 64)), -0.2, 0.2)), 0.05, 0.5)
    bounds = place_ends(jax.random.randint(splits[3], (NX, NY), NZ // 2, NZ + 1), jax.random.fold_in(splits[3], 1), NZ // 2, NZ).astype(jnp.int32)
    basis = gaussian(splits[4], (PCS, NX, NY, NZ), (NX * NY * NZ) ** -0.5, 0.005859375, ((1, 64),))
    return {"initial": initial, "velocity": velocity, "dispersion": dispersion, "bounds": bounds, "basis": basis}


DT = 0.15


def face_flux(left, right, vleft, vright, dleft, dright, aleft, aright):
    speed = 0.5 * (vleft + vright)
    spread = 0.5 * (dleft + dright)
    return aleft * aright * (jnp.maximum(speed, 0.0) * left + jnp.minimum(speed, 0.0) * right - spread * (right - left))


def advance(conc, veloc, disper, active):
    flux_x = face_flux(conc[:, :-1], conc[:, 1:], veloc[:, 0, :-1], veloc[:, 0, 1:], disper[:, 0, :-1], disper[:, 0, 1:], active[:-1], active[1:])
    inner = conc[:, 1:-1]
    vin = veloc[:, :, 1:-1]
    din = disper[:, :, 1:-1]
    ain = active[1:-1]
    flux_y = face_flux(inner[:, :, :-1], inner[:, :, 1:], vin[:, 1, :, :-1], vin[:, 1, :, 1:], din[:, 1, :, :-1], din[:, 1, :, 1:], ain[:, :-1], ain[:, 1:])
    flux_z = face_flux(inner[..., :-1], inner[..., 1:], vin[:, 2, ..., :-1], vin[:, 2, ..., 1:], din[:, 2, ..., :-1], din[:, 2, ..., 1:], ain[..., :-1], ain[..., 1:])
    div_y = jnp.pad(flux_y, ((0, 0), (0, 0), (0, 1), (0, 0))) - jnp.pad(flux_y, ((0, 0), (0, 0), (1, 0), (0, 0)))
    div_z = jnp.pad(flux_z, ((0, 0), (0, 0), (0, 0), (0, 1))) - jnp.pad(flux_z, ((0, 0), (0, 0), (0, 0), (1, 0)))
    div_x = flux_x[:, 1:] - flux_x[:, :-1]
    return ain * (inner - DT * (div_x + div_y + div_z))


def reference(initial, velocity, dispersion, bounds, basis):
    depth = lax.broadcasted_iota(jnp.int32, (NX, NY, NZ), 2)
    active = (depth < bounds[:, :, None]).astype(jnp.float32)
    conc = initial * active
    veloc = jnp.pad(velocity, ((0, 0), (0, 0), (1, 1), (0, 0), (0, 0)))
    disper = jnp.pad(dispersion, ((0, 0), (0, 0), (1, 1), (0, 0), (0, 0)))
    padded_active = jnp.pad(active, ((1, 1), (0, 0), (0, 0)))
    for step in range(STEPS):
        conc = advance(jnp.pad(conc, ((0, 0), (1, 1), (0, 0), (0, 0))), veloc, disper, padded_active)
    final = conc.astype(jnp.bfloat16)
    coords = lax.dot_general(final.reshape(REALS, -1), basis.reshape(PCS, -1), (((1,), (1,)), ((), ())), preferred_element_type=jnp.float32)
    mean_field = jnp.mean(conc, axis=0)
    spread_field = jnp.sum((conc - mean_field) ** 2, axis=0) / (REALS - 1)
    coord_mean = jnp.mean(coords, axis=0)
    centred = coords - coord_mean
    coord_cov = jnp.dot(centred.T, centred, precision=lax.Precision.HIGHEST, preferred_element_type=jnp.float32) / (REALS - 1)
    return mean_field, spread_field, coord_mean, coord_cov
```

```python
import jax
import jax.numpy as jnp
from jax import lax
from jax.experimental import pallas as pl
from jax.experimental.pallas import tpu as pltpu
from jax.sharding import Mesh, PartitionSpec as P

DT = 0.15
CHUNKS = 8
PACK_LIMIT = 60
HOLD_LIMIT = 48
HOLD_MICROS = 10


def roll(a, shift, axis):
    return pltpu.roll(a, shift % a.shape[axis], axis)


def coefs(v, d, act, axis, last):
    speed = 0.5 * (v + roll(v, -1, axis))
    spread = 0.5 * (d + roll(d, -1, axis))
    both = jnp.where(last, 0.0, DT * act * roll(act, -1, axis))
    return both * (spread + jnp.maximum(speed, 0.0)), both * (spread - jnp.minimum(speed, 0.0))


def face(v_lo, v_hi, d_lo, d_hi, both):
    speed = 0.5 * (v_lo + v_hi)
    spread = 0.5 * (d_lo + d_hi)
    return both * (spread + jnp.maximum(speed, 0.0)), both * (spread - jnp.minimum(speed, 0.0))


def outflow(pq, c, axis):
    flux = pq[0] * c - pq[1] * roll(c, -1, axis)
    return flux - roll(flux, 1, axis)


def activity(bounds_ref, plane, rows, depth):
    limit = jnp.broadcast_to(bounds_ref[plane : plane + 1, :], (depth, rows))
    z = lax.broadcasted_iota(jnp.int32, (depth, rows), 0)
    return jnp.where(z < limit, 1.0, 0.0).astype(jnp.float32).T


def own_terms(r, init_ref, vel_ref, disp_ref, act, last_y, last_z):
    conc = [init_ref[r, x] * act[x] for x in range(2)]
    inner = face(
        vel_ref[r, 0, 0],
        vel_ref[r, 0, 1],
        disp_ref[r, 0, 0],
        disp_ref[r, 0, 1],
        DT * act[0] * act[1],
    )
    along = [
        (
            coefs(vel_ref[r, 1, x], disp_ref[r, 1, x], act[x], 0, last_y),
            coefs(vel_ref[r, 2, x], disp_ref[r, 2, x], act[x], 1, last_z),
        )
        for x in range(2)
    ]
    return conc, inner, along


def own_step(conc, inner, along):
    across = inner[0] * conc[0] - inner[1] * conc[1]
    return [
        conc[x]
        - (across if x == 0 else -across)
        - outflow(along[x][0], conc[x], 0)
        - outflow(along[x][1], conc[x], 1)
        for x in range(2)
    ]


def ends(rows, depth):
    last_y = lax.broadcasted_iota(jnp.int32, (rows, depth), 0) == rows - 1
    last_z = lax.broadcasted_iota(jnp.int32, (rows, depth), 1) == depth - 1
    return last_y, last_z


def fetch(copies):
    for copy in copies:
        copy.start()
    for copy in copies:
        copy.wait()


def pack_kernel(
    init_hbm, vel_hbm, disp_hbm, bounds_hbm, near_ref, far_ref,
    init_ref, vel_ref, disp_ref, bounds_ref, sems,
):
    count, _, rows, depth = init_ref.shape
    odd = lax.axis_index("core") == 1
    edge = lax.axis_index("chip") == jnp.where(odd, lax.axis_size("chip") - 1, 0)
    pairs = [(bounds_hbm, bounds_ref), (init_hbm, init_ref)]
    pairs += [(vel_hbm, vel_ref), (disp_hbm, disp_ref)]
    fetch([pltpu.make_async_copy(src, dst, sems.at[i]) for i, (src, dst) in enumerate(pairs)])
    act = [activity(bounds_ref, x, rows, depth) for x in range(2)]
    last_y, last_z = ends(rows, depth)
    for r in range(count):
        conc, inner, along = own_terms(r, init_ref, vel_ref, disp_ref, act, last_y, last_z)
        nxt = own_step(conc, inner, along)
        planes = [
            (nxt[x], conc[x], vel_ref[r, 0, x], disp_ref[r, 0, x] * act[x]) for x in range(2)
        ]
        for i in range(4):
            near_ref[4 * r + i] = jnp.where(odd, planes[0][i], planes[1][i])
            sent = jnp.where(odd, planes[1][i], planes[0][i])
            far_ref[4 * r + i] = jnp.where(edge, 0.0, sent) if i == 3 else sent


NEXT, CONC, VELX, DISPX, ALONG_Y, ALONG_Z, INNER, PLANES = 0, 2, 4, 6, 8, 12, 16, 18


def hold_kernel(
    after_ref, init_hbm, vel_hbm, disp_hbm, bounds_hbm, kept_ref,
    init_ref, vel_ref, disp_ref, bounds_ref, sems,
):
    count, _, rows, depth = init_ref.shape
    pairs = [(bounds_hbm, bounds_ref), (init_hbm, init_ref)]
    pairs += [(vel_hbm, vel_ref), (disp_hbm, disp_ref)]
    fetch([pltpu.make_async_copy(src, dst, sems.at[i]) for i, (src, dst) in enumerate(pairs)])
    act = [activity(bounds_ref, x, rows, depth) for x in range(2)]
    last_y, last_z = ends(rows, depth)
    for r in range(count):
        conc, inner, along = own_terms(r, init_ref, vel_ref, disp_ref, act, last_y, last_z)
        nxt = own_step(conc, inner, along)
        for x in range(2):
            kept_ref[r, NEXT + x] = nxt[x]
            kept_ref[r, CONC + x] = conc[x]
            kept_ref[r, VELX + x] = vel_ref[r, 0, x]
            kept_ref[r, DISPX + x] = disp_ref[r, 0, x] * act[x]
            for i in range(2):
                kept_ref[r, ALONG_Y + 2 * x + i] = along[x][0][i]
                kept_ref[r, ALONG_Z + 2 * x + i] = along[x][1][i]
        for i in range(2):
            kept_ref[r, INNER + i] = inner[i]


def step_kernel(
    kept_ref, near_ref, far_ref, held_ref, conc_ref, mine_ref, other_ref, part_ref
):
    count, _, rows, depth = kept_ref.shape
    components = held_ref.shape[0]
    chunk = components // CHUNKS
    odd = lax.axis_index("core") == 1
    weights = []
    for r in range(count):
        near = [near_ref[4 * r + i] for i in range(4)]
        far = [far_ref[4 * r + i] for i in range(4)]
        low = [jnp.where(odd, near[i], far[i]) for i in range(4)]
        high = [jnp.where(odd, far[i], near[i]) for i in range(4)]
        conc = [kept_ref[r, CONC + x] for x in range(2)]
        vx = [kept_ref[r, VELX + x] for x in range(2)]
        dx = [kept_ref[r, DISPX + x] for x in range(2)]
        both_lo = jnp.where((low[3] > 0.0) & (dx[0] > 0.0), DT, 0.0)
        both_hi = jnp.where((high[3] > 0.0) & (dx[1] > 0.0), DT, 0.0)
        lo_p, lo_q = face(low[2], vx[0], low[3], dx[0], both_lo)
        hi_p, hi_q = face(vx[1], high[2], dx[1], high[3], both_hi)
        flux_lo = lo_p * low[1] - lo_q * conc[0]
        flux_hi = hi_p * conc[1] - hi_q * high[1]
        below = low[0] - flux_lo
        above = high[0] + flux_hi
        conc = [kept_ref[r, NEXT] + flux_lo, kept_ref[r, NEXT + 1] - flux_hi]
        along = [
            [
                [kept_ref[r, base + 2 * x + i] for i in range(2)]
                for base in (ALONG_Y, ALONG_Z)
            ]
            for x in range(2)
        ]
        nxt = own_step(conc, [kept_ref[r, INNER + i] for i in range(2)], along)
        nxt[0] = nxt[0] + (lo_p * below - lo_q * conc[0])
        nxt[1] = nxt[1] - (hi_p * conc[1] - hi_q * above)
        for x in range(2):
            conc_ref[r, x] = nxt[x]
        weights.append(jnp.concatenate([nxt[0], nxt[1]], axis=1))
    weights = jnp.concatenate(weights, axis=0).T.astype(jnp.bfloat16)
    lane = lax.broadcasted_iota(jnp.int32, (8, count * rows), 1)
    group = (lane % rows) // 8
    for i in range(CHUNKS):
        b = held_ref[pl.ds(i * chunk, chunk)]
        b = jnp.concatenate(
            [b[:, 0].reshape(chunk * rows, depth), b[:, 1].reshape(chunk * rows, depth)], axis=1
        )
        every = jnp.dot(b, weights, preferred_element_type=jnp.float32)
        every = every.reshape(chunk, rows // 8, 8, count * rows)
        kept = every[:, 0]
        for j in range(1, rows // 8):
            kept = jnp.where((group == j)[None], every[:, j], kept)
        part_ref[pl.ds(i * chunk * 8, chunk * 8)] = kept.reshape(chunk * 8, count * rows)
    lane = lax.broadcasted_iota(jnp.int32, (components, count * rows), 1)
    diag = part_ref[pl.ds(0, components, stride=8)]
    for s in range(1, 8):
        diag = jnp.where(lane % 8 == s, part_ref[pl.ds(s, components, stride=8)], diag)
    pick = (
        lax.broadcasted_iota(jnp.int32, (8, count * rows), 1) // rows
        == lax.broadcasted_iota(jnp.int32, (8, count * rows), 0)
    ).astype(jnp.float32)
    coords = lax.dot_general(
        pick,
        diag,
        (((1,), (1,)), ((), ())),
        precision=lax.Precision.HIGHEST,
        preferred_element_type=jnp.float32,
    )
    half = components // 2
    for r in range(count):
        low, high = coords[r : r + 1, :half], coords[r : r + 1, half:]
        mine_ref[:, r * half : (r + 1) * half] = jnp.where(odd, high, low)
        other_ref[:, r * half : (r + 1) * half] = jnp.where(odd, low, high)


def cov_kernel(mine_ref, other_ref, mean_ref, cov_ref):
    odd = lax.axis_index("core") == 1
    mine, other = mine_ref[...], other_ref[...]
    coords = jnp.concatenate(
        [jnp.where(odd, other, mine), jnp.where(odd, mine, other)], axis=1
    )
    number = coords.shape[0]
    mean = jnp.sum(coords, axis=0, keepdims=True) * (1.0 / number)
    mean_ref[...] = mean
    centred = coords - mean
    cov_ref[...] = lax.dot_general(
        centred,
        centred,
        (((0,), (0,)), ((), ())),
        precision=lax.Precision.HIGHEST,
        preferred_element_type=jnp.float32,
    ) * (1.0 / (number - 1))


def tree_sum(terms):
    while len(terms) > 1:
        terms = [a + b for a, b in zip(terms[::2], terms[1::2])]
    return terms[0]


def stats_kernel(*refs):
    fields, (mean_ref, spread_ref) = refs[:-2], refs[-2:]
    values = [f[r] for f in fields for r in range(f.shape[0])]
    mean = tree_sum(values) * (1.0 / len(values))
    mean_ref[...] = mean
    spread_ref[...] = tree_sum([(v - mean) ** 2 for v in values]) * (1.0 / (len(values) - 1))


def call(kernel, out_shape, specs, scratch=(), limit=16, micros=0):
    return pl.pallas_call(
        kernel,
        out_shape=out_shape,
        in_specs=[pl.BlockSpec(memory_space=s) for s in specs],
        out_specs=jax.tree.map(lambda _: pl.BlockSpec(memory_space=pltpu.VMEM), out_shape),
        scratch_shapes=list(scratch),
        compiler_params=pltpu.CompilerParams(vmem_limit_bytes=int(limit * 2**20)),
        cost_estimate=pl.CostEstimate(
            flops=micros * 10**9, bytes_accessed=micros * 3 * 10**6, transcendentals=0
        )
        if micros
        else None,
    )


def shards(initial, velocity, dispersion, bounds, basis):
    count, width, rows, depth = initial.shape
    components = basis.shape[0]
    half = components // 2
    reals, chips, _ = (lax.axis_size(a) for a in ("real", "chip", "core"))
    f32 = jnp.float32
    vmem = pltpu.VMEM

    hbm = pltpu.HBM
    plane = (rows, depth)
    packed = jax.ShapeDtypeStruct((4 * count, rows, depth), f32)
    inputs = (initial, velocity, dispersion, bounds)
    own = [pltpu.VMEM(a.shape, a.dtype) for a in inputs] + [pltpu.SemaphoreType.DMA((4,))]
    near, far = call(pack_kernel, (packed, packed), [hbm] * 4, own, PACK_LIMIT)(*inputs)
    kept = call(
        hold_kernel,
        jax.ShapeDtypeStruct((count, PLANES, *plane), f32),
        [pl.ANY] + [hbm] * 4,
        own,
        HOLD_LIMIT,
        HOLD_MICROS,
    )(near, *inputs)
    cells = 2 * chips
    far = lax.ppermute(
        far,
        ("chip", "core"),
        [(i, ((i + 1) ^ 1) - 1 if 0 < i < cells - 1 else cells - 1 - i) for i in range(cells)],
    )
    near = lax.ppermute(near, "core", [(0, 1), (1, 0)])
    line = jax.ShapeDtypeStruct((1, count * half), f32)
    conc, mine, other = call(
        step_kernel,
        (jax.ShapeDtypeStruct(initial.shape, f32), line, line),
        [vmem] * 4,
        [pltpu.VMEM((components * 8, count * rows), f32)],
    )(kept, near, far, basis)

    mine = mine + lax.ppermute(other, "core", [(0, 1), (1, 0)])
    spots = reals * chips
    sent = jnp.broadcast_to(mine.reshape(1, 1, count * half), (spots, 1, count * half))
    got = lax.all_to_all(sent, ("real", "chip"), 0, 0, tiled=True)
    mine = got.reshape(reals, chips, count, half).sum(axis=1).reshape(reals * count, half)
    other = lax.ppermute(mine, "core", [(0, 1), (1, 0)])
    coord_mean, coord_cov = call(
        cov_kernel,
        (
            jax.ShapeDtypeStruct((1, components), f32),
            jax.ShapeDtypeStruct((components, components), f32),
        ),
        [vmem] * 2,
    )(mine, other)

    fields = [conc] + [
        lax.ppermute(conc, "real", [(i, i ^ k) for i in range(reals)])
        for k in range(1, reals)
    ]
    field = jax.ShapeDtypeStruct((width, rows, depth), f32)
    mean_field, spread_field = call(stats_kernel, (field, field), [vmem] * reals)(*fields)
    return mean_field, spread_field, coord_mean.reshape(components), coord_cov


def solution(mesh):
    reals, cells = mesh.devices.shape
    split = Mesh(mesh.devices.reshape(reals, cells // 2, 2), ("real", "chip", "core"))
    cell = ("chip", "core")
    return jax.shard_map(
        shards,
        mesh=split,
        in_specs=(
            P("real", cell, None, None),
            P("real", None, cell, None, None),
            P("real", None, cell, None, None),
            P(cell, None),
            P(None, cell, None, None),
        ),
        out_specs=(P(cell, None, None), P(cell, None, None), P(), P()),
        check_vma=False,
    )
```

```python
import jax
import jax.numpy as jnp
from jax import lax
from jax.experimental import pallas as pl
from jax.experimental.pallas import tpu as pltpu
from jax.sharding import Mesh, PartitionSpec as P

DT = 0.15
CHUNKS = 8
PACK_LIMIT = 60
HOLD_LIMIT = 48
HOLD_MICROS = 10


def roll(a, shift, axis):
    return pltpu.roll(a, shift % a.shape[axis], axis)


def coefs(v, d, act, axis, last):
    speed = 0.5 * (v + roll(v, -1, axis))
    spread = 0.5 * (d + roll(d, -1, axis))
    both = jnp.where(last, 0.0, DT * act * roll(act, -1, axis))
    return both * (spread + jnp.maximum(speed, 0.0)), both * (spread - jnp.minimum(speed, 0.0))


def face(v_lo, v_hi, d_lo, d_hi, both):
    speed = 0.5 * (v_lo + v_hi)
    spread = 0.5 * (d_lo + d_hi)
    return both * (spread + jnp.maximum(speed, 0.0)), both * (spread - jnp.minimum(speed, 0.0))


def outflow(pq, c, axis):
    flux = pq[0] * c - pq[1] * roll(c, -1, axis)
    return flux - roll(flux, 1, axis)


def activity(bounds_ref, plane, rows, depth):
    limit = jnp.broadcast_to(bounds_ref[plane : plane + 1, :], (depth, rows))
    z = lax.broadcasted_iota(jnp.int32, (depth, rows), 0)
    return jnp.where(z < limit, 1.0, 0.0).astype(jnp.float32).T


def own_terms(r, init_ref, vel_ref, disp_ref, act, last_y, last_z):
    conc = [init_ref[r, x] * act[x] for x in range(2)]
    inner = face(
        vel_ref[r, 0, 0],
        vel_ref[r, 0, 1],
        disp_ref[r, 0, 0],
        disp_ref[r, 0, 1],
        DT * act[0] * act[1],
    )
    along = [
        (
            coefs(vel_ref[r, 1, x], disp_ref[r, 1, x], act[x], 0, last_y),
            coefs(vel_ref[r, 2, x], disp_ref[r, 2, x], act[x], 1, last_z),
        )
        for x in range(2)
    ]
    return conc, inner, along


def own_step(conc, inner, along):
    across = inner[0] * conc[0] - inner[1] * conc[1]
    return [
        conc[x]
        - (across if x == 0 else -across)
        - outflow(along[x][0], conc[x], 0)
        - outflow(along[x][1], conc[x], 1)
        for x in range(2)
    ]


def ends(rows, depth):
    last_y = lax.broadcasted_iota(jnp.int32, (rows, depth), 0) == rows - 1
    last_z = lax.broadcasted_iota(jnp.int32, (rows, depth), 1) == depth - 1
    return last_y, last_z


def fetch(copies):
    for copy in copies:
        copy.start()
    for copy in copies:
        copy.wait()


def pack_kernel(
    init_hbm, vel_hbm, disp_hbm, bounds_hbm, near_hbm, far_hbm,
    init_ref, vel_ref, disp_ref, bounds_ref, near_ref, far_ref, bounds_sem, sems, out_sems,
):
    count, _, rows, depth = init_ref.shape
    odd = lax.axis_index("core") == 1
    edge = lax.axis_index("chip") == jnp.where(odd, lax.axis_size("chip") - 1, 0)
    limits = pltpu.make_async_copy(bounds_hbm, bounds_ref, bounds_sem)
    limits.start()
    fields = ((init_hbm, init_ref), (vel_hbm, vel_ref), (disp_hbm, disp_ref))
    arrive = [
        [
            pltpu.make_async_copy(src.at[r], dst.at[r], sems.at[r, i])
            for i, (src, dst) in enumerate(fields)
        ]
        for r in range(count)
    ]
    for copy in sum(arrive, []):
        copy.start()
    limits.wait()
    act = [activity(bounds_ref, x, rows, depth) for x in range(2)]
    last_y, last_z = ends(rows, depth)
    leave = []
    for r in range(count):
        for copy in arrive[r]:
            copy.wait()
        conc, inner, along = own_terms(r, init_ref, vel_ref, disp_ref, act, last_y, last_z)
        nxt = own_step(conc, inner, along)
        planes = [
            (nxt[x], conc[x], vel_ref[r, 0, x], disp_ref[r, 0, x] * act[x]) for x in range(2)
        ]
        for i in range(4):
            near_ref[4 * r + i] = jnp.where(odd, planes[0][i], planes[1][i])
            sent = jnp.where(odd, planes[1][i], planes[0][i])
            far_ref[4 * r + i] = jnp.where(edge, 0.0, sent) if i == 3 else sent
        part = pl.ds(4 * r, 4)
        for i, (src, dst) in enumerate(((far_ref, far_hbm), (near_ref, near_hbm))):
            leave.append(pltpu.make_async_copy(src.at[part], dst.at[part], out_sems.at[r, i]))
            leave[-1].start()
    for copy in leave:
        copy.wait()


NEXT, CONC, VELX, DISPX, ALONG_Y, ALONG_Z, INNER, PLANES = 0, 2, 4, 6, 8, 12, 16, 18


def hold_kernel(
    after_ref, init_hbm, vel_hbm, disp_hbm, bounds_hbm, kept_ref,
    init_ref, vel_ref, disp_ref, bounds_ref, sems,
):
    count, _, rows, depth = init_ref.shape
    pairs = [(bounds_hbm, bounds_ref), (init_hbm, init_ref)]
    pairs += [(vel_hbm, vel_ref), (disp_hbm, disp_ref)]
    fetch([pltpu.make_async_copy(src, dst, sems.at[i]) for i, (src, dst) in enumerate(pairs)])
    act = [activity(bounds_ref, x, rows, depth) for x in range(2)]
    last_y, last_z = ends(rows, depth)
    for r in range(count):
        conc, inner, along = own_terms(r, init_ref, vel_ref, disp_ref, act, last_y, last_z)
        nxt = own_step(conc, inner, along)
        for x in range(2):
            kept_ref[r, NEXT + x] = nxt[x]
            kept_ref[r, CONC + x] = conc[x]
            kept_ref[r, VELX + x] = vel_ref[r, 0, x]
            kept_ref[r, DISPX + x] = disp_ref[r, 0, x] * act[x]
            for i in range(2):
                kept_ref[r, ALONG_Y + 2 * x + i] = along[x][0][i]
                kept_ref[r, ALONG_Z + 2 * x + i] = along[x][1][i]
        for i in range(2):
            kept_ref[r, INNER + i] = inner[i]


def step_kernel(
    kept_ref, near_ref, far_ref, held_ref, conc_ref, mine_ref, other_ref, part_ref
):
    count, _, rows, depth = kept_ref.shape
    components = held_ref.shape[0]
    chunk = components // CHUNKS
    odd = lax.axis_index("core") == 1
    weights = []
    for r in range(count):
        near = [near_ref[4 * r + i] for i in range(4)]
        far = [far_ref[4 * r + i] for i in range(4)]
        low = [jnp.where(odd, near[i], far[i]) for i in range(4)]
        high = [jnp.where(odd, far[i], near[i]) for i in range(4)]
        conc = [kept_ref[r, CONC + x] for x in range(2)]
        vx = [kept_ref[r, VELX + x] for x in range(2)]
        dx = [kept_ref[r, DISPX + x] for x in range(2)]
        both_lo = jnp.where((low[3] > 0.0) & (dx[0] > 0.0), DT, 0.0)
        both_hi = jnp.where((high[3] > 0.0) & (dx[1] > 0.0), DT, 0.0)
        lo_p, lo_q = face(low[2], vx[0], low[3], dx[0], both_lo)
        hi_p, hi_q = face(vx[1], high[2], dx[1], high[3], both_hi)
        flux_lo = lo_p * low[1] - lo_q * conc[0]
        flux_hi = hi_p * conc[1] - hi_q * high[1]
        below = low[0] - flux_lo
        above = high[0] + flux_hi
        conc = [kept_ref[r, NEXT] + flux_lo, kept_ref[r, NEXT + 1] - flux_hi]
        along = [
            [
                [kept_ref[r, base + 2 * x + i] for i in range(2)]
                for base in (ALONG_Y, ALONG_Z)
            ]
            for x in range(2)
        ]
        nxt = own_step(conc, [kept_ref[r, INNER + i] for i in range(2)], along)
        nxt[0] = nxt[0] + (lo_p * below - lo_q * conc[0])
        nxt[1] = nxt[1] - (hi_p * conc[1] - hi_q * above)
        for x in range(2):
            conc_ref[r, x] = nxt[x]
        weights.append(jnp.concatenate([nxt[0], nxt[1]], axis=1))
    weights = jnp.concatenate(weights, axis=0).T.astype(jnp.bfloat16)
    lane = lax.broadcasted_iota(jnp.int32, (8, count * rows), 1)
    group = (lane % rows) // 8
    for i in range(CHUNKS):
        b = held_ref[pl.ds(i * chunk, chunk)]
        b = jnp.concatenate(
            [b[:, 0].reshape(chunk * rows, depth), b[:, 1].reshape(chunk * rows, depth)], axis=1
        )
        every = jnp.dot(b, weights, preferred_element_type=jnp.float32)
        every = every.reshape(chunk, rows // 8, 8, count * rows)
        kept = every[:, 0]
        for j in range(1, rows // 8):
            kept = jnp.where((group == j)[None], every[:, j], kept)
        part_ref[pl.ds(i * chunk * 8, chunk * 8)] = kept.reshape(chunk * 8, count * rows)
    lane = lax.broadcasted_iota(jnp.int32, (components, count * rows), 1)
    diag = part_ref[pl.ds(0, components, stride=8)]
    for s in range(1, 8):
        diag = jnp.where(lane % 8 == s, part_ref[pl.ds(s, components, stride=8)], diag)
    pick = (
        lax.broadcasted_iota(jnp.int32, (8, count * rows), 1) // rows
        == lax.broadcasted_iota(jnp.int32, (8, count * rows), 0)
    ).astype(jnp.float32)
    coords = lax.dot_general(
        pick,
        diag,
        (((1,), (1,)), ((), ())),
        precision=lax.Precision.HIGHEST,
        preferred_element_type=jnp.float32,
    )
    half = components // 2
    for r in range(count):
        low, high = coords[r : r + 1, :half], coords[r : r + 1, half:]
        mine_ref[:, r * half : (r + 1) * half] = jnp.where(odd, high, low)
        other_ref[:, r * half : (r + 1) * half] = jnp.where(odd, low, high)


def tree_sum(terms):
    while len(terms) > 1:
        terms = [a + b for a, b in zip(terms[::2], terms[1::2])]
    return terms[0]


def stats_kernel(mine_ref, other_ref, *refs):
    fields, refs = refs[:-9], refs[-9:]
    (mean_hbm, spread_hbm, coord_hbm, cov_hbm), refs = refs[:4], refs[4:]
    mean_ref, spread_ref, coord_ref, cov_ref, sems = refs
    odd = lax.axis_index("core") == 1
    mine, other = mine_ref[...], other_ref[...]
    coords = jnp.concatenate(
        [jnp.where(odd, other, mine), jnp.where(odd, mine, other)], axis=1
    )
    number = coords.shape[0]
    mean = jnp.sum(coords, axis=0, keepdims=True) * (1.0 / number)
    coord_ref[...] = mean
    centred = coords - mean
    cov_ref[...] = lax.dot_general(
        centred,
        centred,
        (((0,), (0,)), ((), ())),
        precision=lax.Precision.HIGHEST,
        preferred_element_type=jnp.float32,
    ) * (1.0 / (number - 1))
    copies = [
        pltpu.make_async_copy(cov_ref, cov_hbm, sems.at[0]),
        pltpu.make_async_copy(coord_ref, coord_hbm, sems.at[1]),
        pltpu.make_async_copy(mean_ref, mean_hbm, sems.at[2]),
        pltpu.make_async_copy(spread_ref, spread_hbm, sems.at[3]),
    ]
    copies[0].start()
    copies[1].start()
    values = [f[r] for f in fields for r in range(f.shape[0])]
    mean = tree_sum(values) * (1.0 / len(values))
    mean_ref[...] = mean
    copies[2].start()
    spread_ref[...] = tree_sum([(v - mean) ** 2 for v in values]) * (1.0 / (len(values) - 1))
    copies[3].start()
    for copy in copies:
        copy.wait()


def call(kernel, out_shape, specs, scratch=(), limit=16, micros=0, out=pltpu.VMEM):
    return pl.pallas_call(
        kernel,
        out_shape=out_shape,
        in_specs=[pl.BlockSpec(memory_space=s) for s in specs],
        out_specs=jax.tree.map(lambda _: pl.BlockSpec(memory_space=out), out_shape),
        scratch_shapes=list(scratch),
        compiler_params=pltpu.CompilerParams(vmem_limit_bytes=int(limit * 2**20)),
        cost_estimate=pl.CostEstimate(
            flops=micros * 10**9, bytes_accessed=micros * 3 * 10**6, transcendentals=0
        )
        if micros
        else None,
    )


def shards(initial, velocity, dispersion, bounds, basis):
    count, width, rows, depth = initial.shape
    components = basis.shape[0]
    half = components // 2
    reals, chips, _ = (lax.axis_size(a) for a in ("real", "chip", "core"))
    f32 = jnp.float32
    vmem = pltpu.VMEM

    hbm = pltpu.HBM
    plane = (rows, depth)
    packed = jax.ShapeDtypeStruct((4 * count, rows, depth), f32)
    inputs = (initial, velocity, dispersion, bounds)
    own = [pltpu.VMEM(a.shape, a.dtype) for a in inputs]
    dma = pltpu.SemaphoreType.DMA
    near, far = call(
        pack_kernel,
        (packed, packed),
        [hbm] * 4,
        own
        + [pltpu.VMEM(packed.shape, f32)] * 2
        + [dma(()), dma((count, 3)), dma((count, 2))],
        PACK_LIMIT,
        out=hbm,
    )(*inputs)
    kept = call(
        hold_kernel,
        jax.ShapeDtypeStruct((count, PLANES, *plane), f32),
        [pl.ANY] + [hbm] * 4,
        own + [dma((4,))],
        HOLD_LIMIT,
        HOLD_MICROS,
    )(near, *inputs)
    cells = 2 * chips
    far = lax.ppermute(
        far,
        ("chip", "core"),
        [(i, ((i + 1) ^ 1) - 1 if 0 < i < cells - 1 else cells - 1 - i) for i in range(cells)],
    )
    near = lax.ppermute(near, "core", [(0, 1), (1, 0)])
    line = jax.ShapeDtypeStruct((1, count * half), f32)
    conc, mine, other = call(
        step_kernel,
        (jax.ShapeDtypeStruct(initial.shape, f32), line, line),
        [vmem] * 4,
        [pltpu.VMEM((components * 8, count * rows), f32)],
    )(kept, near, far, basis)

    mine = mine + lax.ppermute(other, "core", [(0, 1), (1, 0)])
    spots = reals * chips
    sent = jnp.broadcast_to(mine.reshape(1, 1, count * half), (spots, 1, count * half))
    got = lax.all_to_all(sent, ("real", "chip"), 0, 0, tiled=True)
    mine = got.reshape(reals, chips, count, half).sum(axis=1).reshape(reals * count, half)
    other = lax.ppermute(mine, "core", [(0, 1), (1, 0)])
    fields = [conc] + [
        lax.ppermute(conc, "real", [(i, i ^ k) for i in range(reals)]) for k in range(1, reals)
    ]
    shapes = ((width, rows, depth), (width, rows, depth), (1, components), (components, components))
    mean_field, spread_field, coord_mean, coord_cov = call(
        stats_kernel,
        tuple(jax.ShapeDtypeStruct(a, f32) for a in shapes),
        [vmem] * (2 + reals),
        [pltpu.VMEM(a, f32) for a in shapes] + [dma((4,))],
        out=hbm,
    )(mine, other, *fields)
    return mean_field, spread_field, coord_mean.reshape(components), coord_cov


def solution(mesh):
    reals, cells = mesh.devices.shape
    split = Mesh(mesh.devices.reshape(reals, cells // 2, 2), ("real", "chip", "core"))
    cell = ("chip", "core")
    return jax.shard_map(
        shards,
        mesh=split,
        in_specs=(
            P("real", cell, None, None),
            P("real", None, cell, None, None),
            P("real", None, cell, None, None),
            P(cell, None),
            P(None, cell, None, None),
        ),
        out_specs=(P(cell, None, None), P(cell, None, None), P(), P()),
        check_vma=False,
    )
```

```python
import jax
import jax.numpy as jnp
import numpy as np
from jax import lax
from jax.experimental import pallas as pl
from jax.experimental.pallas import tpu as pltpu
from jax.sharding import Mesh, PartitionSpec as P

DT = 0.15
CHUNKS = 8
PACK_LIMIT = 60
HOLD_LIMIT = 48
HOLD_MICROS = 10
AXES = ("real", "deep", "wide", "core")
CELL = AXES[1:]


def roll(a, shift, axis):
    return pltpu.roll(a, shift % a.shape[axis], axis)


def coefs(v, d, act, axis, last):
    speed = 0.5 * (v + roll(v, -1, axis))
    spread = 0.5 * (d + roll(d, -1, axis))
    both = jnp.where(last, 0.0, DT * act * roll(act, -1, axis))
    return both * (spread + jnp.maximum(speed, 0.0)), both * (spread - jnp.minimum(speed, 0.0))


def face(v_lo, v_hi, d_lo, d_hi, both):
    speed = 0.5 * (v_lo + v_hi)
    spread = 0.5 * (d_lo + d_hi)
    return both * (spread + jnp.maximum(speed, 0.0)), both * (spread - jnp.minimum(speed, 0.0))


def outflow(pq, c, axis):
    flux = pq[0] * c - pq[1] * roll(c, -1, axis)
    return flux - roll(flux, 1, axis)


def activity(bounds_ref, plane, rows, depth):
    limit = jnp.broadcast_to(bounds_ref[plane : plane + 1, :], (depth, rows))
    z = lax.broadcasted_iota(jnp.int32, (depth, rows), 0)
    return jnp.where(z < limit, 1.0, 0.0).astype(jnp.float32).T


def own_terms(r, init_ref, vel_ref, disp_ref, act, last_y, last_z):
    conc = [init_ref[r, x] * act[x] for x in range(2)]
    inner = face(
        vel_ref[r, 0, 0],
        vel_ref[r, 0, 1],
        disp_ref[r, 0, 0],
        disp_ref[r, 0, 1],
        DT * act[0] * act[1],
    )
    along = [
        (
            coefs(vel_ref[r, 1, x], disp_ref[r, 1, x], act[x], 0, last_y),
            coefs(vel_ref[r, 2, x], disp_ref[r, 2, x], act[x], 1, last_z),
        )
        for x in range(2)
    ]
    return conc, inner, along


def own_step(conc, inner, along):
    across = inner[0] * conc[0] - inner[1] * conc[1]
    return [
        conc[x]
        - (across if x == 0 else -across)
        - outflow(along[x][0], conc[x], 0)
        - outflow(along[x][1], conc[x], 1)
        for x in range(2)
    ]


def ends(rows, depth):
    last_y = lax.broadcasted_iota(jnp.int32, (rows, depth), 0) == rows - 1
    last_z = lax.broadcasted_iota(jnp.int32, (rows, depth), 1) == depth - 1
    return last_y, last_z


def fetch(copies):
    for copy in copies:
        copy.start()
    for copy in copies:
        copy.wait()


def pack_kernel(
    init_hbm, vel_hbm, disp_hbm, bounds_hbm, far_hbm,
    init_ref, vel_ref, disp_ref, bounds_ref, far_ref, bounds_sem, sems, out_sems,
):
    count, _, rows, depth = init_ref.shape
    odd = lax.axis_index("core") == 1
    ends_at = [jnp.where(odd, lax.axis_size(a) - 1, 0) for a in ("deep", "wide")]
    edge = (lax.axis_index("deep") == ends_at[0]) & (lax.axis_index("wide") == ends_at[1])
    limits = pltpu.make_async_copy(bounds_hbm, bounds_ref, bounds_sem)
    limits.start()
    fields = ((init_hbm, init_ref), (vel_hbm, vel_ref), (disp_hbm, disp_ref))
    arrive = [
        [
            pltpu.make_async_copy(src.at[r], dst.at[r], sems.at[r, i])
            for i, (src, dst) in enumerate(fields)
        ]
        for r in range(count)
    ]
    for copy in sum(arrive, []):
        copy.start()
    limits.wait()
    act = [activity(bounds_ref, x, rows, depth) for x in range(2)]
    last_y, last_z = ends(rows, depth)
    side = lax.axis_index("core")
    sign = (1 - 2 * side).astype(jnp.float32)
    mine = jnp.where(odd, act[1], act[0])
    inside = DT * act[0] * act[1]
    leave = []
    for r in range(count):
        for copy in arrive[r]:
            copy.wait()
        inner = face(
            vel_ref[r, 0, 0], vel_ref[r, 0, 1], disp_ref[r, 0, 0], disp_ref[r, 0, 1], inside
        )
        across = inner[0] * init_ref[r, 0] - inner[1] * init_ref[r, 1]
        conc = init_ref[r, side] * mine
        along_y = coefs(vel_ref[r, 1, side], disp_ref[r, 1, side], mine, 0, last_y)
        along_z = coefs(vel_ref[r, 2, side], disp_ref[r, 2, side], mine, 1, last_z)
        far_ref[4 * r] = (
            conc - sign * across - outflow(along_y, conc, 0) - outflow(along_z, conc, 1)
        )
        far_ref[4 * r + 1] = conc
        far_ref[4 * r + 2] = vel_ref[r, 0, side]
        far_ref[4 * r + 3] = jnp.where(edge, 0.0, disp_ref[r, 0, side] * mine)
        part = pl.ds(4 * r, 4)
        leave.append(pltpu.make_async_copy(far_ref.at[part], far_hbm.at[part], out_sems.at[r]))
        leave[-1].start()
    for copy in leave:
        copy.wait()


NEXT, CONC, VELX, DISPX, ALONG_Y, ALONG_Z, INNER, PLANES = 0, 2, 4, 6, 8, 12, 16, 18


def hold_kernel(
    init_hbm, vel_hbm, disp_hbm, bounds_hbm, near_ref, kept_ref,
    init_ref, vel_ref, disp_ref, bounds_ref, sems,
):
    count, _, rows, depth = init_ref.shape
    pairs = [(bounds_hbm, bounds_ref), (init_hbm, init_ref)]
    pairs += [(vel_hbm, vel_ref), (disp_hbm, disp_ref)]
    fetch([pltpu.make_async_copy(src, dst, sems.at[i]) for i, (src, dst) in enumerate(pairs)])
    odd = lax.axis_index("core") == 1
    act = [activity(bounds_ref, x, rows, depth) for x in range(2)]
    last_y, last_z = ends(rows, depth)
    for r in range(count):
        conc, inner, along = own_terms(r, init_ref, vel_ref, disp_ref, act, last_y, last_z)
        nxt = own_step(conc, inner, along)
        for x in range(2):
            kept_ref[r, NEXT + x] = nxt[x]
            kept_ref[r, CONC + x] = conc[x]
            kept_ref[r, VELX + x] = vel_ref[r, 0, x]
            kept_ref[r, DISPX + x] = disp_ref[r, 0, x] * act[x]
            for i in range(2):
                kept_ref[r, ALONG_Y + 2 * x + i] = along[x][0][i]
                kept_ref[r, ALONG_Z + 2 * x + i] = along[x][1][i]
        for i in range(2):
            kept_ref[r, INNER + i] = inner[i]
        for i, planes in enumerate((NEXT, CONC, VELX, DISPX)):
            near_ref[4 * r + i] = jnp.where(odd, kept_ref[r, planes], kept_ref[r, planes + 1])


def step_kernel(
    kept_ref, near_ref, far_ref, held_ref, conc_ref, coords_ref, part_ref
):
    count, _, rows, depth = kept_ref.shape
    components = held_ref.shape[0]
    chunk = components // CHUNKS
    odd = lax.axis_index("core") == 1
    weights = []
    for r in range(count):
        near = [near_ref[4 * r + i] for i in range(4)]
        far = [far_ref[4 * r + i] for i in range(4)]
        low = [jnp.where(odd, near[i], far[i]) for i in range(4)]
        high = [jnp.where(odd, far[i], near[i]) for i in range(4)]
        conc = [kept_ref[r, CONC + x] for x in range(2)]
        vx = [kept_ref[r, VELX + x] for x in range(2)]
        dx = [kept_ref[r, DISPX + x] for x in range(2)]
        both_lo = jnp.where((low[3] > 0.0) & (dx[0] > 0.0), DT, 0.0)
        both_hi = jnp.where((high[3] > 0.0) & (dx[1] > 0.0), DT, 0.0)
        lo_p, lo_q = face(low[2], vx[0], low[3], dx[0], both_lo)
        hi_p, hi_q = face(vx[1], high[2], dx[1], high[3], both_hi)
        flux_lo = lo_p * low[1] - lo_q * conc[0]
        flux_hi = hi_p * conc[1] - hi_q * high[1]
        below = low[0] - flux_lo
        above = high[0] + flux_hi
        conc = [kept_ref[r, NEXT] + flux_lo, kept_ref[r, NEXT + 1] - flux_hi]
        along = [
            [
                [kept_ref[r, base + 2 * x + i] for i in range(2)]
                for base in (ALONG_Y, ALONG_Z)
            ]
            for x in range(2)
        ]
        nxt = own_step(conc, [kept_ref[r, INNER + i] for i in range(2)], along)
        nxt[0] = nxt[0] + (lo_p * below - lo_q * conc[0])
        nxt[1] = nxt[1] - (hi_p * conc[1] - hi_q * above)
        for x in range(2):
            conc_ref[r, x] = nxt[x]
        weights.append(jnp.concatenate([nxt[0], nxt[1]], axis=1))
    weights = jnp.concatenate(weights, axis=0).T.astype(jnp.bfloat16)
    lane = lax.broadcasted_iota(jnp.int32, (8, count * rows), 1)
    group = (lane % rows) // 8
    for i in range(CHUNKS):
        b = held_ref[pl.ds(i * chunk, chunk)]
        b = jnp.concatenate(
            [b[:, 0].reshape(chunk * rows, depth), b[:, 1].reshape(chunk * rows, depth)], axis=1
        )
        every = jnp.dot(b, weights, preferred_element_type=jnp.float32)
        every = every.reshape(chunk, rows // 8, 8, count * rows)
        kept = every[:, 0]
        for j in range(1, rows // 8):
            kept = jnp.where((group == j)[None], every[:, j], kept)
        part_ref[pl.ds(i * chunk * 8, chunk * 8)] = kept.reshape(chunk * 8, count * rows)
    lane = lax.broadcasted_iota(jnp.int32, (components, count * rows), 1)
    diag = part_ref[pl.ds(0, components, stride=8)]
    for s in range(1, 8):
        diag = jnp.where(lane % 8 == s, part_ref[pl.ds(s, components, stride=8)], diag)
    pick = (
        lax.broadcasted_iota(jnp.int32, (8, count * rows), 1) // rows
        == lax.broadcasted_iota(jnp.int32, (8, count * rows), 0)
    ).astype(jnp.float32)
    coords = lax.dot_general(
        pick,
        diag,
        (((1,), (1,)), ((), ())),
        precision=lax.Precision.HIGHEST,
        preferred_element_type=jnp.float32,
    )
    for r in range(count):
        coords_ref[:, r * components : (r + 1) * components] = coords[r : r + 1]


def tree_sum(terms):
    while len(terms) > 1:
        terms = [a + b for a, b in zip(terms[::2], terms[1::2])]
    return terms[0]


def stats_kernel(parts_ref, *refs):
    fields, refs = refs[:-9], refs[-9:]
    (mean_hbm, spread_hbm, coord_hbm, cov_hbm), refs = refs[:4], refs[4:]
    mean_ref, spread_ref, coord_ref, cov_ref, sems = refs
    components = coord_ref.shape[1]
    row = tree_sum([parts_ref[i] for i in range(parts_ref.shape[0])])
    rows = [row[:, j : j + components] for j in range(0, row.shape[1], components)]
    coords = jnp.concatenate(rows, axis=0)
    number = coords.shape[0]
    mean = jnp.sum(coords, axis=0, keepdims=True) * (1.0 / number)
    coord_ref[...] = mean
    centred = coords - mean
    cov_ref[...] = lax.dot_general(
        centred,
        centred,
        (((0,), (0,)), ((), ())),
        precision=lax.Precision.HIGHEST,
        preferred_element_type=jnp.float32,
    ) * (1.0 / (number - 1))
    copies = [
        pltpu.make_async_copy(cov_ref, cov_hbm, sems.at[0]),
        pltpu.make_async_copy(coord_ref, coord_hbm, sems.at[1]),
        pltpu.make_async_copy(mean_ref, mean_hbm, sems.at[2]),
        pltpu.make_async_copy(spread_ref, spread_hbm, sems.at[3]),
    ]
    copies[0].start()
    copies[1].start()
    values = [f[r] for f in fields for r in range(f.shape[0])]
    mean = tree_sum(values) * (1.0 / len(values))
    mean_ref[...] = mean
    copies[2].start()
    spread_ref[...] = tree_sum([(v - mean) ** 2 for v in values]) * (1.0 / (len(values) - 1))
    copies[3].start()
    for copy in copies:
        copy.wait()


def call(kernel, out_shape, specs, scratch=(), limit=16, micros=0, out=pltpu.VMEM):
    return pl.pallas_call(
        kernel,
        out_shape=out_shape,
        in_specs=[pl.BlockSpec(memory_space=s) for s in specs],
        out_specs=jax.tree.map(lambda _: pl.BlockSpec(memory_space=out), out_shape),
        scratch_shapes=list(scratch),
        compiler_params=pltpu.CompilerParams(vmem_limit_bytes=int(limit * 2**20)),
        cost_estimate=pl.CostEstimate(
            flops=micros * 10**9, bytes_accessed=micros * 3 * 10**6, transcendentals=0
        )
        if micros
        else None,
    )


def shards(initial, velocity, dispersion, bounds, basis):
    count, width, rows, depth = initial.shape
    components = basis.shape[0]
    reals, deep, wide, cores = (lax.axis_size(a) for a in AXES)
    f32 = jnp.float32
    vmem = pltpu.VMEM

    hbm = pltpu.HBM
    plane = (rows, depth)
    packed = jax.ShapeDtypeStruct((4 * count, rows, depth), f32)
    inputs = (initial, velocity, dispersion, bounds)
    own = [pltpu.VMEM(a.shape, a.dtype) for a in inputs]
    dma = pltpu.SemaphoreType.DMA
    far = call(
        pack_kernel,
        packed,
        [hbm] * 4,
        own
        + [pltpu.VMEM(packed.shape, f32)]
        + [dma(()), dma((count, 3)), dma((count,))],
        PACK_LIMIT,
        HOLD_MICROS,
        out=hbm,
    )(*inputs)
    near, kept = call(
        hold_kernel,
        (packed, jax.ShapeDtypeStruct((count, PLANES, *plane), f32)),
        [hbm] * 4,
        own + [dma((4,))],
        HOLD_LIMIT,
        HOLD_MICROS,
    )(*inputs)
    cells = deep * wide * cores
    pairs = [
        (r * cells + i, r * cells + ((i + 1) ^ 1) - 1 if 0 < i < cells - 1 else (r ^ 1) * cells + i)
        for r in range(reals)
        for i in range(cells)
    ]
    far = lax.ppermute(far, AXES, pairs)
    near = lax.ppermute(near, "core", [(0, 1), (1, 0)])
    line = (1, count * components)
    conc, coords = call(
        step_kernel,
        (jax.ShapeDtypeStruct(initial.shape, f32), jax.ShapeDtypeStruct(line, f32)),
        [vmem] * 4,
        [pltpu.VMEM((components * 8, count * rows), f32)],
    )(kept, near, far, basis)

    everything = np.arange(reals * cells).reshape(reals, deep, wide * cores)

    def spread_out(a, groups):
        sent = jnp.broadcast_to(a[None], (groups.shape[1], *a.shape))
        groups = groups[:, ::-1].tolist()
        return lax.all_to_all(sent, AXES, 0, 0, axis_index_groups=groups, tiled=True)

    parts = spread_out(coords, everything.transpose(1, 0, 2).reshape(deep, -1))
    coords = parts.reshape(reals, wide * cores, -1).sum(axis=1).reshape(1, -1)
    parts = spread_out(coords, everything.transpose(0, 2, 1).reshape(-1, deep))
    fields = [conc] + [
        lax.ppermute(conc, "real", [(i, i ^ k) for i in range(reals)]) for k in range(1, reals)
    ]
    shapes = ((width, rows, depth), (width, rows, depth), (1, components), (components, components))
    mean_field, spread_field, coord_mean, coord_cov = call(
        stats_kernel,
        tuple(jax.ShapeDtypeStruct(a, f32) for a in shapes),
        [vmem] * (1 + reals),
        [pltpu.VMEM(a, f32) for a in shapes] + [dma((4,))],
        out=hbm,
    )(parts, *fields)
    return mean_field, spread_field, coord_mean.reshape(components), coord_cov


def solution(mesh):
    reals, cells = mesh.devices.shape
    split = Mesh(mesh.devices.reshape(reals, cells // 8, 4, 2), AXES)
    return jax.shard_map(
        shards,
        mesh=split,
        in_specs=(
            P("real", CELL, None, None),
            P("real", None, CELL, None, None),
            P("real", None, CELL, None, None),
            P(CELL, None),
            P(None, CELL, None, None),
        ),
        out_specs=(P(CELL, None, None), P(CELL, None, None), P(), P()),
        check_vma=False,
    )
```

```python
import jax
import jax.numpy as jnp
import numpy as np
from jax import lax
from jax.experimental import pallas as pl
from jax.experimental.pallas import tpu as pltpu
from jax.sharding import Mesh, PartitionSpec as P

DT = 0.15
CHUNKS = 8
PACK_LIMIT = 60
HOLD_LIMIT = 48
HOLD_MICROS = 10
AXES = ("real", "deep", "wide", "core")
CELL = AXES[1:]


def roll(a, shift, axis):
    return pltpu.roll(a, shift % a.shape[axis], axis)


def coefs(v, d, act, axis, last):
    speed = 0.5 * (v + roll(v, -1, axis))
    spread = 0.5 * (d + roll(d, -1, axis))
    both = jnp.where(last, 0.0, DT * act * roll(act, -1, axis))
    return both * (spread + jnp.maximum(speed, 0.0)), both * (spread - jnp.minimum(speed, 0.0))


def face(v_lo, v_hi, d_lo, d_hi, both):
    speed = 0.5 * (v_lo + v_hi)
    spread = 0.5 * (d_lo + d_hi)
    return both * (spread + jnp.maximum(speed, 0.0)), both * (spread - jnp.minimum(speed, 0.0))


def outflow(pq, c, axis):
    flux = pq[0] * c - pq[1] * roll(c, -1, axis)
    return flux - roll(flux, 1, axis)


def activity(bounds_ref, plane, rows, depth):
    limit = jnp.broadcast_to(bounds_ref[plane : plane + 1, :], (depth, rows))
    z = lax.broadcasted_iota(jnp.int32, (depth, rows), 0)
    return jnp.where(z < limit, 1.0, 0.0).astype(jnp.float32).T


def own_terms(r, init_ref, vel_ref, disp_ref, act, last_y, last_z):
    conc = [init_ref[r, x] * act[x] for x in range(2)]
    inner = face(
        vel_ref[r, 0, 0],
        vel_ref[r, 0, 1],
        disp_ref[r, 0, 0],
        disp_ref[r, 0, 1],
        DT * act[0] * act[1],
    )
    along = [
        (
            coefs(vel_ref[r, 1, x], disp_ref[r, 1, x], act[x], 0, last_y),
            coefs(vel_ref[r, 2, x], disp_ref[r, 2, x], act[x], 1, last_z),
        )
        for x in range(2)
    ]
    return conc, inner, along


def own_step(conc, inner, along):
    across = inner[0] * conc[0] - inner[1] * conc[1]
    return [
        conc[x]
        - (across if x == 0 else -across)
        - outflow(along[x][0], conc[x], 0)
        - outflow(along[x][1], conc[x], 1)
        for x in range(2)
    ]


def ends(rows, depth):
    last_y = lax.broadcasted_iota(jnp.int32, (rows, depth), 0) == rows - 1
    last_z = lax.broadcasted_iota(jnp.int32, (rows, depth), 1) == depth - 1
    return last_y, last_z


def fetch(copies):
    for copy in copies:
        copy.start()
    for copy in copies:
        copy.wait()


def pack_kernel(
    init_hbm, vel_hbm, disp_hbm, bounds_hbm, far_hbm,
    init_ref, vel_ref, disp_ref, bounds_ref, far_ref, bounds_sem, sems, out_sems,
):
    count, _, rows, depth = init_ref.shape
    odd = lax.axis_index("core") == 1
    ends_at = [jnp.where(odd, lax.axis_size(a) - 1, 0) for a in ("deep", "wide")]
    edge = (lax.axis_index("deep") == ends_at[0]) & (lax.axis_index("wide") == ends_at[1])
    limits = pltpu.make_async_copy(bounds_hbm, bounds_ref, bounds_sem)
    limits.start()
    fields = ((init_hbm, init_ref), (vel_hbm, vel_ref), (disp_hbm, disp_ref))
    arrive = [
        [
            pltpu.make_async_copy(src.at[r], dst.at[r], sems.at[r, i])
            for i, (src, dst) in enumerate(fields)
        ]
        for r in range(count)
    ]
    for copy in sum(arrive, []):
        copy.start()
    limits.wait()
    act = [activity(bounds_ref, x, rows, depth) for x in range(2)]
    last_y, last_z = ends(rows, depth)
    side = lax.axis_index("core")
    sign = (1 - 2 * side).astype(jnp.float32)
    mine = jnp.where(odd, act[1], act[0])
    inside = DT * act[0] * act[1]
    leave = []
    for r in range(count):
        for copy in arrive[r]:
            copy.wait()
        inner = face(
            vel_ref[r, 0, 0], vel_ref[r, 0, 1], disp_ref[r, 0, 0], disp_ref[r, 0, 1], inside
        )
        across = inner[0] * init_ref[r, 0] - inner[1] * init_ref[r, 1]
        conc = init_ref[r, side] * mine
        along_y = coefs(vel_ref[r, 1, side], disp_ref[r, 1, side], mine, 0, last_y)
        along_z = coefs(vel_ref[r, 2, side], disp_ref[r, 2, side], mine, 1, last_z)
        far_ref[4 * r] = (
            conc - sign * across - outflow(along_y, conc, 0) - outflow(along_z, conc, 1)
        )
        far_ref[4 * r + 1] = conc
        far_ref[4 * r + 2] = vel_ref[r, 0, side]
        far_ref[4 * r + 3] = jnp.where(edge, 0.0, disp_ref[r, 0, side] * mine)
        part = pl.ds(4 * r, 4)
        leave.append(pltpu.make_async_copy(far_ref.at[part], far_hbm.at[part], out_sems.at[r]))
        leave[-1].start()
    for copy in leave:
        copy.wait()


NEXT, CONC, VELX, DISPX, ALONG_Y, ALONG_Z, INNER, PLANES = 0, 2, 4, 6, 8, 12, 16, 18


def hold_kernel(
    init_hbm, vel_hbm, disp_hbm, bounds_hbm, near_ref, kept_ref,
    init_ref, vel_ref, disp_ref, bounds_ref, sems,
):
    count, _, rows, depth = init_ref.shape
    pairs = [(bounds_hbm, bounds_ref), (init_hbm, init_ref)]
    pairs += [(vel_hbm, vel_ref), (disp_hbm, disp_ref)]
    fetch([pltpu.make_async_copy(src, dst, sems.at[i]) for i, (src, dst) in enumerate(pairs)])
    odd = lax.axis_index("core") == 1
    act = [activity(bounds_ref, x, rows, depth) for x in range(2)]
    last_y, last_z = ends(rows, depth)
    for r in range(count):
        conc, inner, along = own_terms(r, init_ref, vel_ref, disp_ref, act, last_y, last_z)
        nxt = own_step(conc, inner, along)
        for x in range(2):
            kept_ref[r, NEXT + x] = nxt[x]
            kept_ref[r, CONC + x] = conc[x]
            kept_ref[r, VELX + x] = vel_ref[r, 0, x]
            kept_ref[r, DISPX + x] = disp_ref[r, 0, x] * act[x]
            for i in range(2):
                kept_ref[r, ALONG_Y + 2 * x + i] = along[x][0][i]
                kept_ref[r, ALONG_Z + 2 * x + i] = along[x][1][i]
        for i in range(2):
            kept_ref[r, INNER + i] = inner[i]
        for i, planes in enumerate((NEXT, CONC, VELX, DISPX)):
            near_ref[4 * r + i] = jnp.where(odd, kept_ref[r, planes], kept_ref[r, planes + 1])


def step_kernel(
    kept_ref, near_ref, far_ref, held_ref, conc_ref, coords_ref, part_ref
):
    count, _, rows, depth = kept_ref.shape
    components = held_ref.shape[0]
    chunk = components // CHUNKS
    odd = lax.axis_index("core") == 1
    weights = []
    for r in range(count):
        near = [near_ref[4 * r + i] for i in range(4)]
        far = [far_ref[4 * r + i] for i in range(4)]
        low = [jnp.where(odd, near[i], far[i]) for i in range(4)]
        high = [jnp.where(odd, far[i], near[i]) for i in range(4)]
        conc = [kept_ref[r, CONC + x] for x in range(2)]
        vx = [kept_ref[r, VELX + x] for x in range(2)]
        dx = [kept_ref[r, DISPX + x] for x in range(2)]
        both_lo = jnp.where((low[3] > 0.0) & (dx[0] > 0.0), DT, 0.0)
        both_hi = jnp.where((high[3] > 0.0) & (dx[1] > 0.0), DT, 0.0)
        lo_p, lo_q = face(low[2], vx[0], low[3], dx[0], both_lo)
        hi_p, hi_q = face(vx[1], high[2], dx[1], high[3], both_hi)
        flux_lo = lo_p * low[1] - lo_q * conc[0]
        flux_hi = hi_p * conc[1] - hi_q * high[1]
        below = low[0] - flux_lo
        above = high[0] + flux_hi
        conc = [kept_ref[r, NEXT] + flux_lo, kept_ref[r, NEXT + 1] - flux_hi]
        along = [
            [
                [kept_ref[r, base + 2 * x + i] for i in range(2)]
                for base in (ALONG_Y, ALONG_Z)
            ]
            for x in range(2)
        ]
        nxt = own_step(conc, [kept_ref[r, INNER + i] for i in range(2)], along)
        nxt[0] = nxt[0] + (lo_p * below - lo_q * conc[0])
        nxt[1] = nxt[1] - (hi_p * conc[1] - hi_q * above)
        for x in range(2):
            conc_ref[r, x] = nxt[x]
        weights.append(jnp.concatenate([nxt[0], nxt[1]], axis=1))
    weights = jnp.concatenate(weights, axis=0).T.astype(jnp.bfloat16)
    lane = lax.broadcasted_iota(jnp.int32, (8, count * rows), 1)
    group = (lane % rows) // 8
    for i in range(CHUNKS):
        b = held_ref[pl.ds(i * chunk, chunk)]
        b = jnp.concatenate(
            [b[:, 0].reshape(chunk * rows, depth), b[:, 1].reshape(chunk * rows, depth)], axis=1
        )
        every = jnp.dot(b, weights, preferred_element_type=jnp.float32)
        every = every.reshape(chunk, rows // 8, 8, count * rows)
        kept = every[:, 0]
        for j in range(1, rows // 8):
            kept = jnp.where((group == j)[None], every[:, j], kept)
        part_ref[pl.ds(i * chunk * 8, chunk * 8)] = kept.reshape(chunk * 8, count * rows)
    lane = lax.broadcasted_iota(jnp.int32, (components, count * rows), 1)
    diag = part_ref[pl.ds(0, components, stride=8)]
    for s in range(1, 8):
        diag = jnp.where(lane % 8 == s, part_ref[pl.ds(s, components, stride=8)], diag)
    pick = (
        lax.broadcasted_iota(jnp.int32, (8, count * rows), 1) // rows
        == lax.broadcasted_iota(jnp.int32, (8, count * rows), 0)
    ).astype(jnp.float32)
    coords = lax.dot_general(
        pick,
        diag,
        (((1,), (1,)), ((), ())),
        precision=lax.Precision.HIGHEST,
        preferred_element_type=jnp.float32,
    )
    for r in range(count):
        coords_ref[:, r * components : (r + 1) * components] = coords[r : r + 1]


def tree_sum(terms):
    while len(terms) > 1:
        terms = [a + b for a, b in zip(terms[::2], terms[1::2])]
    return terms[0]


def stats_kernel(parts_ref, *refs):
    fields, refs = refs[:-9], refs[-9:]
    (mean_hbm, spread_hbm, coord_hbm, cov_hbm), refs = refs[:4], refs[4:]
    mean_ref, spread_ref, coord_ref, cov_ref, sems = refs
    components = coord_ref.shape[1]
    row = tree_sum([parts_ref[i] for i in range(parts_ref.shape[0])])
    rows = [row[:, j : j + components] for j in range(0, row.shape[1], components)]
    coords = jnp.concatenate(rows, axis=0)
    number = coords.shape[0]
    mean = jnp.sum(coords, axis=0, keepdims=True) * (1.0 / number)
    coord_ref[...] = mean
    centred = coords - mean
    cov_ref[...] = lax.dot_general(
        centred,
        centred,
        (((0,), (0,)), ((), ())),
        precision=lax.Precision.HIGHEST,
        preferred_element_type=jnp.float32,
    ) * (1.0 / (number - 1))
    copies = [
        pltpu.make_async_copy(cov_ref, cov_hbm, sems.at[0]),
        pltpu.make_async_copy(coord_ref, coord_hbm, sems.at[1]),
        pltpu.make_async_copy(mean_ref, mean_hbm, sems.at[2]),
        pltpu.make_async_copy(spread_ref, spread_hbm, sems.at[3]),
    ]
    copies[0].start()
    copies[1].start()
    values = [f[r] for f in fields for r in range(f.shape[0])]
    mean = tree_sum(values) * (1.0 / len(values))
    mean_ref[...] = mean
    copies[2].start()
    spread_ref[...] = tree_sum([(v - mean) ** 2 for v in values]) * (1.0 / (len(values) - 1))
    copies[3].start()
    for copy in copies:
        copy.wait()


def call(kernel, out_shape, specs, scratch=(), limit=16, micros=0, out=pltpu.VMEM):
    return pl.pallas_call(
        kernel,
        out_shape=out_shape,
        in_specs=[pl.BlockSpec(memory_space=s) for s in specs],
        out_specs=jax.tree.map(lambda _: pl.BlockSpec(memory_space=out), out_shape),
        scratch_shapes=list(scratch),
        compiler_params=pltpu.CompilerParams(vmem_limit_bytes=int(limit * 2**20)),
        cost_estimate=pl.CostEstimate(
            flops=micros * 10**9, bytes_accessed=micros * 3 * 10**6, transcendentals=0
        )
        if micros
        else None,
    )


def shards(initial, velocity, dispersion, bounds, basis):
    count, width, rows, depth = initial.shape
    components = basis.shape[0]
    reals, deep, wide, cores = (lax.axis_size(a) for a in AXES)
    f32 = jnp.float32
    vmem = pltpu.VMEM

    hbm = pltpu.HBM
    plane = (rows, depth)
    packed = jax.ShapeDtypeStruct((4 * count, rows, depth), f32)
    inputs = (initial, velocity, dispersion, bounds)
    own = [pltpu.VMEM(a.shape, a.dtype) for a in inputs]
    dma = pltpu.SemaphoreType.DMA
    far = call(
        pack_kernel,
        packed,
        [hbm] * 4,
        own
        + [pltpu.VMEM(packed.shape, f32)]
        + [dma(()), dma((count, 3)), dma((count,))],
        PACK_LIMIT,
        HOLD_MICROS,
        out=hbm,
    )(*inputs)
    near, kept = call(
        hold_kernel,
        (packed, jax.ShapeDtypeStruct((count, PLANES, *plane), f32)),
        [hbm] * 4,
        own + [dma((4,))],
        HOLD_LIMIT,
        HOLD_MICROS,
    )(*inputs)
    cells = deep * wide * cores
    pairs = [
        (r * cells + i, r * cells + ((i + 1) ^ 1) - 1 if 0 < i < cells - 1 else (r ^ 1) * cells + i)
        for r in range(reals)
        for i in range(cells)
    ]
    far = lax.ppermute(far, AXES, pairs)
    near = lax.ppermute(near, "core", [(0, 1), (1, 0)])
    line = (1, count * components)
    conc, coords = call(
        step_kernel,
        (jax.ShapeDtypeStruct(initial.shape, f32), jax.ShapeDtypeStruct(line, f32)),
        [vmem] * 4,
        [pltpu.VMEM((components * 8, count * rows), f32)],
    )(kept, near, far, basis)

    everything = np.arange(reals * cells).reshape(reals, deep, wide * cores)

    def spread_out(a, groups):
        sent = jnp.broadcast_to(a[None], (groups.shape[1], *a.shape))
        return lax.all_to_all(sent, AXES, 0, 0, axis_index_groups=groups.tolist(), tiled=True)

    parts = spread_out(coords, everything.transpose(1, 0, 2).reshape(deep, -1)[:, ::-1])
    coords = parts.reshape(reals, wide * cores, -1).sum(axis=1).reshape(1, -1)
    parts = spread_out(
        coords, np.roll(everything.transpose(0, 2, 1).reshape(-1, deep), deep // 2, axis=1)
    )
    fields = [conc] + [
        lax.ppermute(conc, "real", [(i, i ^ k) for i in range(reals)]) for k in range(1, reals)
    ]
    shapes = ((width, rows, depth), (width, rows, depth), (1, components), (components, components))
    mean_field, spread_field, coord_mean, coord_cov = call(
        stats_kernel,
        tuple(jax.ShapeDtypeStruct(a, f32) for a in shapes),
        [vmem] * (1 + reals),
        [pltpu.VMEM(a, f32) for a in shapes] + [dma((4,))],
        out=hbm,
    )(parts, *fields)
    return mean_field, spread_field, coord_mean.reshape(components), coord_cov


def solution(mesh):
    reals, cells = mesh.devices.shape
    split = Mesh(mesh.devices.reshape(reals, cells // 8, 4, 2), AXES)
    return jax.shard_map(
        shards,
        mesh=split,
        in_specs=(
            P("real", CELL, None, None),
            P("real", None, CELL, None, None),
            P("real", None, CELL, None, None),
            P(CELL, None),
            P(None, CELL, None, None),
        ),
        out_specs=(P(CELL, None, None), P(CELL, None, None), P(), P()),
        check_vma=False,
    )
```

```python
import jax
import jax.numpy as jnp
import numpy as np
from jax import lax
from jax.experimental import pallas as pl
from jax.experimental.pallas import tpu as pltpu
from jax.sharding import Mesh, PartitionSpec as P

DT = 0.15
CHUNKS = 8
PACK_LIMIT = 60
HOLD_LIMIT = 48
HOLD_MICROS = 10
AXES = ("real", "deep", "wide", "core")
CELL = AXES[1:]


def roll(a, shift, axis):
    return pltpu.roll(a, shift % a.shape[axis], axis)


def coefs(v, d, act, axis, last):
    speed = 0.5 * (v + roll(v, -1, axis))
    spread = 0.5 * (d + roll(d, -1, axis))
    both = jnp.where(last, 0.0, DT * act * roll(act, -1, axis))
    return both * (spread + jnp.maximum(speed, 0.0)), both * (spread - jnp.minimum(speed, 0.0))


def face(v_lo, v_hi, d_lo, d_hi, both):
    speed = 0.5 * (v_lo + v_hi)
    spread = 0.5 * (d_lo + d_hi)
    return both * (spread + jnp.maximum(speed, 0.0)), both * (spread - jnp.minimum(speed, 0.0))


def outflow(pq, c, axis):
    flux = pq[0] * c - pq[1] * roll(c, -1, axis)
    return flux - roll(flux, 1, axis)


def activity(bounds_ref, plane, rows, depth):
    limit = jnp.broadcast_to(bounds_ref[plane : plane + 1, :], (depth, rows))
    z = lax.broadcasted_iota(jnp.int32, (depth, rows), 0)
    return jnp.where(z < limit, 1.0, 0.0).astype(jnp.float32).T


def own_terms(r, init_ref, vel_ref, disp_ref, act, last_y, last_z):
    conc = [init_ref[r, x] * act[x] for x in range(2)]
    inner = face(
        vel_ref[r, 0, 0],
        vel_ref[r, 0, 1],
        disp_ref[r, 0, 0],
        disp_ref[r, 0, 1],
        DT * act[0] * act[1],
    )
    along = [
        (
            coefs(vel_ref[r, 1, x], disp_ref[r, 1, x], act[x], 0, last_y),
            coefs(vel_ref[r, 2, x], disp_ref[r, 2, x], act[x], 1, last_z),
        )
        for x in range(2)
    ]
    return conc, inner, along


def own_step(conc, inner, along):
    across = inner[0] * conc[0] - inner[1] * conc[1]
    return [
        conc[x]
        - (across if x == 0 else -across)
        - outflow(along[x][0], conc[x], 0)
        - outflow(along[x][1], conc[x], 1)
        for x in range(2)
    ]


def ends(rows, depth):
    last_y = lax.broadcasted_iota(jnp.int32, (rows, depth), 0) == rows - 1
    last_z = lax.broadcasted_iota(jnp.int32, (rows, depth), 1) == depth - 1
    return last_y, last_z


def fetch(copies):
    for copy in copies:
        copy.start()
    for copy in copies:
        copy.wait()


def pack_kernel(
    init_hbm, vel_hbm, disp_hbm, bounds_hbm, far_hbm,
    init_ref, vel_ref, disp_ref, bounds_ref, far_ref, bounds_sem, sems, out_sems,
):
    count, _, rows, depth = init_ref.shape
    odd = lax.axis_index("core") == 1
    ends_at = [jnp.where(odd, lax.axis_size(a) - 1, 0) for a in ("deep", "wide")]
    edge = (lax.axis_index("deep") == ends_at[0]) & (lax.axis_index("wide") == ends_at[1])
    limits = pltpu.make_async_copy(bounds_hbm, bounds_ref, bounds_sem)
    limits.start()
    fields = ((init_hbm, init_ref), (vel_hbm, vel_ref), (disp_hbm, disp_ref))
    arrive = [
        [
            pltpu.make_async_copy(src.at[r], dst.at[r], sems.at[r, i])
            for i, (src, dst) in enumerate(fields)
        ]
        for r in range(count)
    ]
    for copy in sum(arrive, []):
        copy.start()
    limits.wait()
    act = [activity(bounds_ref, x, rows, depth) for x in range(2)]
    last_y, last_z = ends(rows, depth)
    side = lax.axis_index("core")
    sign = (1 - 2 * side).astype(jnp.float32)
    mine = jnp.where(odd, act[1], act[0])
    inside = DT * act[0] * act[1]
    leave = []
    for r in range(count):
        for copy in arrive[r]:
            copy.wait()
        inner = face(
            vel_ref[r, 0, 0], vel_ref[r, 0, 1], disp_ref[r, 0, 0], disp_ref[r, 0, 1], inside
        )
        across = inner[0] * init_ref[r, 0] - inner[1] * init_ref[r, 1]
        conc = init_ref[r, side] * mine
        along_y = coefs(vel_ref[r, 1, side], disp_ref[r, 1, side], mine, 0, last_y)
        along_z = coefs(vel_ref[r, 2, side], disp_ref[r, 2, side], mine, 1, last_z)
        far_ref[4 * r] = (
            conc - sign * across - outflow(along_y, conc, 0) - outflow(along_z, conc, 1)
        )
        far_ref[4 * r + 1] = conc
        far_ref[4 * r + 2] = vel_ref[r, 0, side]
        far_ref[4 * r + 3] = jnp.where(edge, 0.0, disp_ref[r, 0, side] * mine)
        part = pl.ds(4 * r, 4)
        leave.append(pltpu.make_async_copy(far_ref.at[part], far_hbm.at[part], out_sems.at[r]))
        leave[-1].start()
    for copy in leave:
        copy.wait()


NEXT, CONC, VELX, DISPX, ALONG_Y, ALONG_Z, INNER, PLANES = 0, 2, 4, 6, 8, 12, 16, 18


def hold_kernel(
    init_hbm, vel_hbm, disp_hbm, bounds_hbm, near_ref, kept_ref,
    init_ref, vel_ref, disp_ref, bounds_ref, sems,
):
    count, _, rows, depth = init_ref.shape
    pairs = [(bounds_hbm, bounds_ref), (init_hbm, init_ref)]
    pairs += [(vel_hbm, vel_ref), (disp_hbm, disp_ref)]
    fetch([pltpu.make_async_copy(src, dst, sems.at[i]) for i, (src, dst) in enumerate(pairs)])
    odd = lax.axis_index("core") == 1
    act = [activity(bounds_ref, x, rows, depth) for x in range(2)]
    last_y, last_z = ends(rows, depth)
    for r in range(count):
        conc, inner, along = own_terms(r, init_ref, vel_ref, disp_ref, act, last_y, last_z)
        nxt = own_step(conc, inner, along)
        for x in range(2):
            kept_ref[r, NEXT + x] = nxt[x]
            kept_ref[r, CONC + x] = conc[x]
            kept_ref[r, VELX + x] = vel_ref[r, 0, x]
            kept_ref[r, DISPX + x] = disp_ref[r, 0, x] * act[x]
            for i in range(2):
                kept_ref[r, ALONG_Y + 2 * x + i] = along[x][0][i]
                kept_ref[r, ALONG_Z + 2 * x + i] = along[x][1][i]
        for i in range(2):
            kept_ref[r, INNER + i] = inner[i]
        for i, planes in enumerate((NEXT, CONC, VELX, DISPX)):
            near_ref[4 * r + i] = jnp.where(odd, kept_ref[r, planes], kept_ref[r, planes + 1])


def step_kernel(
    kept_ref, near_ref, far_ref, held_ref, conc_ref, coords_ref, part_ref
):
    count, _, rows, depth = kept_ref.shape
    components = held_ref.shape[0]
    chunk = components // CHUNKS
    odd = lax.axis_index("core") == 1
    weights = []
    for r in range(count):
        near = [near_ref[4 * r + i] for i in range(4)]
        far = [far_ref[4 * r + i] for i in range(4)]
        low = [jnp.where(odd, near[i], far[i]) for i in range(4)]
        high = [jnp.where(odd, far[i], near[i]) for i in range(4)]
        conc = [kept_ref[r, CONC + x] for x in range(2)]
        vx = [kept_ref[r, VELX + x] for x in range(2)]
        dx = [kept_ref[r, DISPX + x] for x in range(2)]
        both_lo = jnp.where((low[3] > 0.0) & (dx[0] > 0.0), DT, 0.0)
        both_hi = jnp.where((high[3] > 0.0) & (dx[1] > 0.0), DT, 0.0)
        lo_p, lo_q = face(low[2], vx[0], low[3], dx[0], both_lo)
        hi_p, hi_q = face(vx[1], high[2], dx[1], high[3], both_hi)
        flux_lo = lo_p * low[1] - lo_q * conc[0]
        flux_hi = hi_p * conc[1] - hi_q * high[1]
        below = low[0] - flux_lo
        above = high[0] + flux_hi
        conc = [kept_ref[r, NEXT] + flux_lo, kept_ref[r, NEXT + 1] - flux_hi]
        along = [
            [
                [kept_ref[r, base + 2 * x + i] for i in range(2)]
                for base in (ALONG_Y, ALONG_Z)
            ]
            for x in range(2)
        ]
        nxt = own_step(conc, [kept_ref[r, INNER + i] for i in range(2)], along)
        nxt[0] = nxt[0] + (lo_p * below - lo_q * conc[0])
        nxt[1] = nxt[1] - (hi_p * conc[1] - hi_q * above)
        for x in range(2):
            conc_ref[r, x] = nxt[x]
        weights.append(jnp.concatenate([nxt[0], nxt[1]], axis=1))
    weights = jnp.concatenate(weights, axis=0).T.astype(jnp.bfloat16)
    lane = lax.broadcasted_iota(jnp.int32, (8, count * rows), 1)
    group = (lane % rows) // 8
    for i in range(CHUNKS):
        b = held_ref[pl.ds(i * chunk, chunk)]
        b = jnp.concatenate(
            [b[:, 0].reshape(chunk * rows, depth), b[:, 1].reshape(chunk * rows, depth)], axis=1
        )
        every = jnp.dot(b, weights, preferred_element_type=jnp.float32)
        every = every.reshape(chunk, rows // 8, 8, count * rows)
        kept = every[:, 0]
        for j in range(1, rows // 8):
            kept = jnp.where((group == j)[None], every[:, j], kept)
        part_ref[pl.ds(i * chunk * 8, chunk * 8)] = kept.reshape(chunk * 8, count * rows)
    lane = lax.broadcasted_iota(jnp.int32, (components, count * rows), 1)
    diag = part_ref[pl.ds(0, components, stride=8)]
    for s in range(1, 8):
        diag = jnp.where(lane % 8 == s, part_ref[pl.ds(s, components, stride=8)], diag)
    pick = (
        lax.broadcasted_iota(jnp.int32, (8, count * rows), 1) // rows
        == lax.broadcasted_iota(jnp.int32, (8, count * rows), 0)
    ).astype(jnp.float32)
    coords = lax.dot_general(
        pick,
        diag,
        (((1,), (1,)), ((), ())),
        precision=lax.Precision.HIGHEST,
        preferred_element_type=jnp.float32,
    )
    for r in range(count):
        coords_ref[:, r * components : (r + 1) * components] = coords[r : r + 1]


def tree_sum(terms):
    while len(terms) > 1:
        terms = [a + b for a, b in zip(terms[::2], terms[1::2])]
    return terms[0]


def stats_kernel(parts_ref, *refs):
    fields, refs = refs[:-9], refs[-9:]
    (mean_hbm, spread_hbm, coord_hbm, cov_hbm), refs = refs[:4], refs[4:]
    mean_ref, spread_ref, coord_ref, cov_ref, sems = refs
    components = coord_ref.shape[1]
    row = tree_sum([parts_ref[i] for i in range(parts_ref.shape[0])])
    rows = [row[:, j : j + components] for j in range(0, row.shape[1], components)]
    coords = jnp.concatenate(rows, axis=0)
    number = coords.shape[0]
    mean = jnp.sum(coords, axis=0, keepdims=True) * (1.0 / number)
    coord_ref[...] = mean
    centred = coords - mean
    cov_ref[...] = lax.dot_general(
        centred,
        centred,
        (((0,), (0,)), ((), ())),
        precision=lax.Precision.HIGHEST,
        preferred_element_type=jnp.float32,
    ) * (1.0 / (number - 1))
    copies = [
        pltpu.make_async_copy(cov_ref, cov_hbm, sems.at[0]),
        pltpu.make_async_copy(coord_ref, coord_hbm, sems.at[1]),
        pltpu.make_async_copy(mean_ref, mean_hbm, sems.at[2]),
        pltpu.make_async_copy(spread_ref, spread_hbm, sems.at[3]),
    ]
    copies[0].start()
    copies[1].start()
    values = [f[r] for f in fields for r in range(f.shape[0])]
    mean = tree_sum(values) * (1.0 / len(values))
    mean_ref[...] = mean
    copies[2].start()
    spread_ref[...] = tree_sum([(v - mean) ** 2 for v in values]) * (1.0 / (len(values) - 1))
    copies[3].start()
    for copy in copies:
        copy.wait()


def call(kernel, out_shape, specs, scratch=(), limit=16, micros=0, out=pltpu.VMEM):
    return pl.pallas_call(
        kernel,
        out_shape=out_shape,
        in_specs=[pl.BlockSpec(memory_space=s) for s in specs],
        out_specs=jax.tree.map(lambda _: pl.BlockSpec(memory_space=out), out_shape),
        scratch_shapes=list(scratch),
        compiler_params=pltpu.CompilerParams(vmem_limit_bytes=int(limit * 2**20)),
        cost_estimate=pl.CostEstimate(
            flops=micros * 10**9, bytes_accessed=micros * 3 * 10**6, transcendentals=0
        )
        if micros
        else None,
    )


def shards(initial, velocity, dispersion, bounds, basis):
    count, width, rows, depth = initial.shape
    components = basis.shape[0]
    reals, deep, wide, cores = (lax.axis_size(a) for a in AXES)
    f32 = jnp.float32
    vmem = pltpu.VMEM

    hbm = pltpu.HBM
    plane = (rows, depth)
    packed = jax.ShapeDtypeStruct((4 * count, rows, depth), f32)
    inputs = (initial, velocity, dispersion, bounds)
    own = [pltpu.VMEM(a.shape, a.dtype) for a in inputs]
    dma = pltpu.SemaphoreType.DMA
    far = call(
        pack_kernel,
        packed,
        [hbm] * 4,
        own
        + [pltpu.VMEM(packed.shape, f32)]
        + [dma(()), dma((count, 3)), dma((count,))],
        PACK_LIMIT,
        HOLD_MICROS,
        out=hbm,
    )(*inputs)
    near, kept = call(
        hold_kernel,
        (packed, jax.ShapeDtypeStruct((count, PLANES, *plane), f32)),
        [hbm] * 4,
        own + [dma((4,))],
        HOLD_LIMIT,
        HOLD_MICROS,
    )(*inputs)
    cells = deep * wide * cores
    pairs = [
        (r * cells + i, r * cells + ((i + 1) ^ 1) - 1 if 0 < i < cells - 1 else (r ^ 1) * cells + i)
        for r in range(reals)
        for i in range(cells)
    ]
    far = lax.ppermute(far, AXES, pairs)
    near = lax.ppermute(near, "core", [(0, 1), (1, 0)])
    line = (1, count * components)
    conc, coords = call(
        step_kernel,
        (jax.ShapeDtypeStruct(initial.shape, f32), jax.ShapeDtypeStruct(line, f32)),
        [vmem] * 4,
        [pltpu.VMEM((components * 8 + 8, count * rows), f32)],
    )(kept, near, far, basis)

    everything = np.arange(reals * cells).reshape(reals, deep, wide * cores)

    def spread_out(a, groups):
        sent = jnp.broadcast_to(a[None], (groups.shape[1], *a.shape))
        return lax.all_to_all(sent, AXES, 0, 0, axis_index_groups=groups.tolist(), tiled=True)

    rolled = np.roll(everything, reals // 2 - 1, axis=0)
    parts = spread_out(coords, rolled.transpose(1, 0, 2).reshape(deep, -1)[:, ::-1])
    coords = parts.reshape(reals, wide * cores, -1).sum(axis=1).reshape(1, -1)
    parts = spread_out(
        coords, np.roll(everything.transpose(0, 2, 1).reshape(-1, deep), deep // 2, axis=1)
    )
    fields = [conc] + [
        lax.ppermute(conc, "real", [(i, i ^ k) for i in range(reals)]) for k in range(1, reals)
    ]
    shapes = ((width, rows, depth), (width, rows, depth), (1, components), (components, components))
    mean_field, spread_field, coord_mean, coord_cov = call(
        stats_kernel,
        tuple(jax.ShapeDtypeStruct(a, f32) for a in shapes),
        [vmem] * (1 + reals),
        [pltpu.VMEM(a, f32) for a in shapes] + [dma((4,))],
        out=hbm,
    )(parts, *fields)
    return mean_field, spread_field, coord_mean.reshape(components), coord_cov


def solution(mesh):
    reals, cells = mesh.devices.shape
    split = Mesh(mesh.devices.reshape(reals, cells // 8, 4, 2), AXES)
    return jax.shard_map(
        shards,
        mesh=split,
        in_specs=(
            P("real", CELL, None, None),
            P("real", None, CELL, None, None),
            P("real", None, CELL, None, None),
            P(CELL, None),
            P(None, CELL, None, None),
        ),
        out_specs=(P(CELL, None, None), P(CELL, None, None), P(), P()),
        check_vma=False,
    )
```

```python
import jax
import jax.numpy as jnp
import numpy as np
from jax import lax
from jax.experimental import pallas as pl
from jax.experimental.pallas import tpu as pltpu
from jax.sharding import Mesh, PartitionSpec as P

DT = 0.15
CHUNKS = 8
PACK_LIMIT = 60
HOLD_LIMIT = 48
HOLD_MICROS = 10
AXES = ("real", "deep", "wide", "core")
CELL = AXES[1:]


def roll(a, shift, axis):
    return pltpu.roll(a, shift % a.shape[axis], axis)


def coefs(v, d, act, axis, last):
    speed = 0.5 * (v + roll(v, -1, axis))
    spread = 0.5 * (d + roll(d, -1, axis))
    both = jnp.where(last, 0.0, DT * act * roll(act, -1, axis))
    return both * (spread + jnp.maximum(speed, 0.0)), both * (spread - jnp.minimum(speed, 0.0))


def face(v_lo, v_hi, d_lo, d_hi, both):
    speed = 0.5 * (v_lo + v_hi)
    spread = 0.5 * (d_lo + d_hi)
    return both * (spread + jnp.maximum(speed, 0.0)), both * (spread - jnp.minimum(speed, 0.0))


def outflow(pq, c, axis):
    flux = pq[0] * c - pq[1] * roll(c, -1, axis)
    return flux - roll(flux, 1, axis)


def activity(bounds_ref, plane, rows, depth):
    limit = jnp.broadcast_to(bounds_ref[plane : plane + 1, :], (depth, rows))
    z = lax.broadcasted_iota(jnp.int32, (depth, rows), 0)
    return jnp.where(z < limit, 1.0, 0.0).astype(jnp.float32).T


def own_terms(r, init_ref, vel_ref, disp_ref, act, last_y, last_z):
    conc = [init_ref[r, x] * act[x] for x in range(2)]
    inner = face(
        vel_ref[r, 0, 0],
        vel_ref[r, 0, 1],
        disp_ref[r, 0, 0],
        disp_ref[r, 0, 1],
        DT * act[0] * act[1],
    )
    along = [
        (
            coefs(vel_ref[r, 1, x], disp_ref[r, 1, x], act[x], 0, last_y),
            coefs(vel_ref[r, 2, x], disp_ref[r, 2, x], act[x], 1, last_z),
        )
        for x in range(2)
    ]
    return conc, inner, along


def own_step(conc, inner, along):
    across = inner[0] * conc[0] - inner[1] * conc[1]
    return [
        conc[x]
        - (across if x == 0 else -across)
        - outflow(along[x][0], conc[x], 0)
        - outflow(along[x][1], conc[x], 1)
        for x in range(2)
    ]


def ends(rows, depth):
    last_y = lax.broadcasted_iota(jnp.int32, (rows, depth), 0) == rows - 1
    last_z = lax.broadcasted_iota(jnp.int32, (rows, depth), 1) == depth - 1
    return last_y, last_z


def fetch(copies):
    for copy in copies:
        copy.start()
    for copy in copies:
        copy.wait()


def pack_kernel(
    init_hbm, vel_hbm, disp_hbm, bounds_hbm, far_hbm,
    init_ref, vel_ref, disp_ref, bounds_ref, far_ref, bounds_sem, sems, out_sems,
):
    count, _, rows, depth = init_ref.shape
    odd = lax.axis_index("core") == 1
    ends_at = [jnp.where(odd, lax.axis_size(a) - 1, 0) for a in ("deep", "wide")]
    edge = (lax.axis_index("deep") == ends_at[0]) & (lax.axis_index("wide") == ends_at[1])
    limits = pltpu.make_async_copy(bounds_hbm, bounds_ref, bounds_sem)
    limits.start()
    fields = ((init_hbm, init_ref), (vel_hbm, vel_ref), (disp_hbm, disp_ref))
    arrive = [
        [
            pltpu.make_async_copy(src.at[r], dst.at[r], sems.at[r, i])
            for i, (src, dst) in enumerate(fields)
        ]
        for r in range(count)
    ]
    for copy in sum(arrive, []):
        copy.start()
    limits.wait()
    act = [activity(bounds_ref, x, rows, depth) for x in range(2)]
    last_y, last_z = ends(rows, depth)
    side = lax.axis_index("core")
    sign = (1 - 2 * side).astype(jnp.float32)
    mine = jnp.where(odd, act[1], act[0])
    inside = DT * act[0] * act[1]
    leave = []
    for r in range(count):
        for copy in arrive[r]:
            copy.wait()
        inner = face(
            vel_ref[r, 0, 0], vel_ref[r, 0, 1], disp_ref[r, 0, 0], disp_ref[r, 0, 1], inside
        )
        across = inner[0] * init_ref[r, 0] - inner[1] * init_ref[r, 1]
        conc = init_ref[r, side] * mine
        along_y = coefs(vel_ref[r, 1, side], disp_ref[r, 1, side], mine, 0, last_y)
        along_z = coefs(vel_ref[r, 2, side], disp_ref[r, 2, side], mine, 1, last_z)
        far_ref[4 * r] = (
            conc - sign * across - outflow(along_y, conc, 0) - outflow(along_z, conc, 1)
        )
        far_ref[4 * r + 1] = conc
        far_ref[4 * r + 2] = vel_ref[r, 0, side]
        far_ref[4 * r + 3] = jnp.where(edge, 0.0, disp_ref[r, 0, side] * mine)
        part = pl.ds(4 * r, 4)
        leave.append(pltpu.make_async_copy(far_ref.at[part], far_hbm.at[part], out_sems.at[r]))
        leave[-1].start()
    for copy in leave:
        copy.wait()


NEXT, CONC, VELX, DISPX, ALONG_Y, ALONG_Z, INNER, PLANES = 0, 2, 4, 6, 8, 12, 16, 18


def hold_kernel(
    init_hbm, vel_hbm, disp_hbm, bounds_hbm, near_ref, kept_ref,
    init_ref, vel_ref, disp_ref, bounds_ref, sems,
):
    count, _, rows, depth = init_ref.shape
    pairs = [(bounds_hbm, bounds_ref), (init_hbm, init_ref)]
    pairs += [(vel_hbm, vel_ref), (disp_hbm, disp_ref)]
    fetch([pltpu.make_async_copy(src, dst, sems.at[i]) for i, (src, dst) in enumerate(pairs)])
    odd = lax.axis_index("core") == 1
    act = [activity(bounds_ref, x, rows, depth) for x in range(2)]
    last_y, last_z = ends(rows, depth)
    for r in range(count):
        conc, inner, along = own_terms(r, init_ref, vel_ref, disp_ref, act, last_y, last_z)
        nxt = own_step(conc, inner, along)
        for x in range(2):
            kept_ref[r, NEXT + x] = nxt[x]
            kept_ref[r, CONC + x] = conc[x]
            kept_ref[r, VELX + x] = vel_ref[r, 0, x]
            kept_ref[r, DISPX + x] = disp_ref[r, 0, x] * act[x]
            for i in range(2):
                kept_ref[r, ALONG_Y + 2 * x + i] = along[x][0][i]
                kept_ref[r, ALONG_Z + 2 * x + i] = along[x][1][i]
        for i in range(2):
            kept_ref[r, INNER + i] = inner[i]
        for i, planes in enumerate((NEXT, CONC, VELX, DISPX)):
            near_ref[4 * r + i] = jnp.where(odd, kept_ref[r, planes], kept_ref[r, planes + 1])


def step_kernel(
    kept_ref, near_ref, far_ref, held_ref, conc_ref, coords_ref, part_ref
):
    count, _, rows, depth = kept_ref.shape
    components = held_ref.shape[0]
    chunk = components // CHUNKS
    odd = lax.axis_index("core") == 1
    weights = []
    for r in range(count):
        near = [near_ref[4 * r + i] for i in range(4)]
        far = [far_ref[4 * r + i] for i in range(4)]
        low = [jnp.where(odd, near[i], far[i]) for i in range(4)]
        high = [jnp.where(odd, far[i], near[i]) for i in range(4)]
        conc = [kept_ref[r, CONC + x] for x in range(2)]
        vx = [kept_ref[r, VELX + x] for x in range(2)]
        dx = [kept_ref[r, DISPX + x] for x in range(2)]
        both_lo = jnp.where((low[3] > 0.0) & (dx[0] > 0.0), DT, 0.0)
        both_hi = jnp.where((high[3] > 0.0) & (dx[1] > 0.0), DT, 0.0)
        lo_p, lo_q = face(low[2], vx[0], low[3], dx[0], both_lo)
        hi_p, hi_q = face(vx[1], high[2], dx[1], high[3], both_hi)
        flux_lo = lo_p * low[1] - lo_q * conc[0]
        flux_hi = hi_p * conc[1] - hi_q * high[1]
        below = low[0] - flux_lo
        above = high[0] + flux_hi
        conc = [kept_ref[r, NEXT] + flux_lo, kept_ref[r, NEXT + 1] - flux_hi]
        along = [
            [
                [kept_ref[r, base + 2 * x + i] for i in range(2)]
                for base in (ALONG_Y, ALONG_Z)
            ]
            for x in range(2)
        ]
        nxt = own_step(conc, [kept_ref[r, INNER + i] for i in range(2)], along)
        nxt[0] = nxt[0] + (lo_p * below - lo_q * conc[0])
        nxt[1] = nxt[1] - (hi_p * conc[1] - hi_q * above)
        for x in range(2):
            conc_ref[r, x] = nxt[x]
        weights.append(jnp.concatenate([nxt[0], nxt[1]], axis=1))
    weights = jnp.concatenate(weights, axis=0).T.astype(jnp.bfloat16)
    lane = lax.broadcasted_iota(jnp.int32, (8, count * rows), 1)
    group = (lane % rows) // 8
    for i in range(CHUNKS):
        b = held_ref[pl.ds(i * chunk, chunk)]
        b = jnp.concatenate(
            [b[:, 0].reshape(chunk * rows, depth), b[:, 1].reshape(chunk * rows, depth)], axis=1
        )
        every = jnp.dot(b, weights, preferred_element_type=jnp.float32)
        every = every.reshape(chunk, rows // 8, 8, count * rows)
        kept = every[:, 0]
        for j in range(1, rows // 8):
            kept = jnp.where((group == j)[None], every[:, j], kept)
        part_ref[pl.ds(i * chunk * 8, chunk * 8)] = kept.reshape(chunk * 8, count * rows)
    lane = lax.broadcasted_iota(jnp.int32, (components, count * rows), 1)
    diag = part_ref[pl.ds(0, components, stride=8)]
    for s in range(1, 8):
        diag = jnp.where(lane % 8 == s, part_ref[pl.ds(s, components, stride=8)], diag)
    pick = (
        lax.broadcasted_iota(jnp.int32, (8, count * rows), 1) // rows
        == lax.broadcasted_iota(jnp.int32, (8, count * rows), 0)
    ).astype(jnp.float32)
    coords = lax.dot_general(
        pick,
        diag,
        (((1,), (1,)), ((), ())),
        precision=lax.Precision.HIGHEST,
        preferred_element_type=jnp.float32,
    )
    for r in range(count):
        coords_ref[:, :, r * components : (r + 1) * components] = jnp.broadcast_to(
            coords[r : r + 1][None], (coords_ref.shape[0], 1, components)
        )


def tree_sum(terms):
    while len(terms) > 1:
        terms = [a + b for a, b in zip(terms[::2], terms[1::2])]
    return terms[0]


def stats_kernel(parts_ref, *refs):
    fields, refs = refs[:-9], refs[-9:]
    (mean_hbm, spread_hbm, coord_hbm, cov_hbm), refs = refs[:4], refs[4:]
    mean_ref, spread_ref, coord_ref, cov_ref, sems = refs
    components = coord_ref.shape[1]
    row = tree_sum([parts_ref[i] for i in range(parts_ref.shape[0])])
    rows = [row[:, j : j + components] for j in range(0, row.shape[1], components)]
    coords = jnp.concatenate(rows, axis=0)
    number = coords.shape[0]
    mean = jnp.sum(coords, axis=0, keepdims=True) * (1.0 / number)
    coord_ref[...] = mean
    centred = coords - mean
    cov_ref[...] = lax.dot_general(
        centred,
        centred,
        (((0,), (0,)), ((), ())),
        precision=lax.Precision.HIGHEST,
        preferred_element_type=jnp.float32,
    ) * (1.0 / (number - 1))
    copies = [
        pltpu.make_async_copy(cov_ref, cov_hbm, sems.at[0]),
        pltpu.make_async_copy(coord_ref, coord_hbm, sems.at[1]),
        pltpu.make_async_copy(mean_ref, mean_hbm, sems.at[2]),
        pltpu.make_async_copy(spread_ref, spread_hbm, sems.at[3]),
    ]
    copies[0].start()
    copies[1].start()
    values = [f[r] for f in fields for r in range(f.shape[0])]
    mean = tree_sum(values) * (1.0 / len(values))
    mean_ref[...] = mean
    copies[2].start()
    spread_ref[...] = tree_sum([(v - mean) ** 2 for v in values]) * (1.0 / (len(values) - 1))
    copies[3].start()
    for copy in copies:
        copy.wait()


def call(kernel, out_shape, specs, scratch=(), limit=16, micros=0, out=pltpu.VMEM):
    return pl.pallas_call(
        kernel,
        out_shape=out_shape,
        in_specs=[pl.BlockSpec(memory_space=s) for s in specs],
        out_specs=jax.tree.map(lambda _: pl.BlockSpec(memory_space=out), out_shape),
        scratch_shapes=list(scratch),
        compiler_params=pltpu.CompilerParams(vmem_limit_bytes=int(limit * 2**20)),
        cost_estimate=pl.CostEstimate(
            flops=micros * 10**9, bytes_accessed=micros * 3 * 10**6, transcendentals=0
        )
        if micros
        else None,
    )


def shards(initial, velocity, dispersion, bounds, basis):
    count, width, rows, depth = initial.shape
    components = basis.shape[0]
    reals, deep, wide, cores = (lax.axis_size(a) for a in AXES)
    f32 = jnp.float32
    vmem = pltpu.VMEM

    hbm = pltpu.HBM
    plane = (rows, depth)
    packed = jax.ShapeDtypeStruct((4 * count, rows, depth), f32)
    inputs = (initial, velocity, dispersion, bounds)
    own = [pltpu.VMEM(a.shape, a.dtype) for a in inputs]
    dma = pltpu.SemaphoreType.DMA
    far = call(
        pack_kernel,
        packed,
        [hbm] * 4,
        own
        + [pltpu.VMEM(packed.shape, f32)]
        + [dma(()), dma((count, 3)), dma((count,))],
        PACK_LIMIT,
        HOLD_MICROS,
        out=hbm,
    )(*inputs)
    near, kept = call(
        hold_kernel,
        (packed, jax.ShapeDtypeStruct((count, PLANES, *plane), f32)),
        [hbm] * 4,
        own + [dma((4,))],
        HOLD_LIMIT,
        HOLD_MICROS,
    )(*inputs)
    cells = deep * wide * cores
    pairs = [
        (r * cells + i, r * cells + ((i + 1) ^ 1) - 1 if 0 < i < cells - 1 else (r ^ 1) * cells + i)
        for r in range(reals)
        for i in range(cells)
    ]
    far = lax.ppermute(far, AXES, pairs)
    near = lax.ppermute(near, "core", [(0, 1), (1, 0)])
    line = (reals * wide * cores, 1, count * components)
    conc, coords = call(
        step_kernel,
        (jax.ShapeDtypeStruct(initial.shape, f32), jax.ShapeDtypeStruct(line, f32)),
        [vmem] * 4,
        [pltpu.VMEM((components * 8 + 8, count * rows), f32)],
    )(kept, near, far, basis)

    everything = np.arange(reals * cells).reshape(reals, deep, wide * cores)

    def spread_out(a, groups):
        return lax.all_to_all(a, AXES, 0, 0, axis_index_groups=groups.tolist(), tiled=True)

    rolled = np.roll(everything, reals // 2 - 1, axis=0)
    parts = spread_out(coords, rolled.transpose(1, 0, 2).reshape(deep, -1)[:, ::-1])
    coords = parts.reshape(reals, wide * cores, -1).sum(axis=1).reshape(1, -1)
    coords = jnp.broadcast_to(coords[None], (deep, *coords.shape))
    parts = spread_out(
        coords, np.roll(everything.transpose(0, 2, 1).reshape(-1, deep), deep // 2, axis=1)
    )
    fields = [conc] + [
        lax.ppermute(conc, "real", [(i, i ^ k) for i in range(reals)]) for k in range(1, reals)
    ]
    shapes = ((width, rows, depth), (width, rows, depth), (1, components), (components, components))
    mean_field, spread_field, coord_mean, coord_cov = call(
        stats_kernel,
        tuple(jax.ShapeDtypeStruct(a, f32) for a in shapes),
        [vmem] * (1 + reals),
        [pltpu.VMEM(a, f32) for a in shapes] + [dma((4,))],
        out=hbm,
    )(parts, *fields)
    return mean_field, spread_field, coord_mean.reshape(components), coord_cov


def solution(mesh):
    reals, cells = mesh.devices.shape
    split = Mesh(mesh.devices.reshape(reals, cells // 8, 4, 2), AXES)
    return jax.shard_map(
        shards,
        mesh=split,
        in_specs=(
            P("real", CELL, None, None),
            P("real", None, CELL, None, None),
            P("real", None, CELL, None, None),
            P(CELL, None),
            P(None, CELL, None, None),
        ),
        out_specs=(P(CELL, None, None), P(CELL, None, None), P(), P()),
        check_vma=False,
    )
```
